32 devices in a mesh: section: 4 (over y, x), tensor: 4 (over z), dp: 2 (over core).
Axes of the slice: x: 2, y: 2, z: 4, core: 2. Of those that a mesh axis runs over, the one named last changes fastest.
Arguments:
- tokens: bfloat16 [4, 2048, 1024], P('section', 'dp', 'tensor'), may hold values from -6 to 6
- lengths: int32 [2, 6], P('dp'), may hold values from 1 to 1024, 4096 in all within a row
- gains: float32 [4, 1024], P('section'), may hold values from 0.5 to 1.5
- qk_gains: float32 [2, 64], replicated, may hold values from 0.5 to 1.5
- conv_kernel: bfloat16 [3, 1024], P(None, 'tensor'), may hold values from -3.5 to 3.5
- conv_in: bfloat16 [1024, 3, 1024], P(('section', 'dp'), None, 'tensor'), may hold values from -0.1875 to 0.1875
- conv_out: bfloat16 [1024, 1024], P('tensor', ('section', 'dp')), may hold values from -0.1875 to 0.1875
- ffn1_in: bfloat16 [1024, 2, 4608], P(('section', 'dp'), None, 'tensor'), may hold values from -0.1875 to 0.1875
- ffn1_out: bfloat16 [4608, 1024], P('tensor', ('section', 'dp')), may hold values from -0.09375 to 0.09375
- attn_qkv: bfloat16 [1024, 8, 256], P(('section', 'dp'), 'tensor'), may hold values from -0.1875 to 0.1875
- attn_out: bfloat16 [1024, 1024], P('tensor', ('section', 'dp')), may hold values from -3 to 3
- ffn2_in: bfloat16 [1024, 2, 4608], P(('section', 'dp'), None, 'tensor'), may hold values from -0.1875 to 0.1875
- ffn2_out: bfloat16 [4608, 1024], P('tensor', ('section', 'dp')), may hold values from -0.09375 to 0.09375
- cotangent: bfloat16 [4, 2048, 1024], P('section', 'dp', 'tensor'), may hold values from -6 to 6
Outputs:
- output: bfloat16 [4, 2048, 1024], P('section', 'dp', 'tensor')
- input_grad: bfloat16 [4, 2048, 1024], P('section', 'dp', 'tensor')
- gains_grad: float32 [4, 1024], replicated
- qk_gains_grad: float32 [2, 64], replicated
- conv_kernel_grad: float32 [3, 1024], replicated
- conv_in_grad: float32 [1024, 3, 1024], P(('section', 'dp'), None, 'tensor')
- conv_out_grad: float32 [1024, 1024], P('tensor', ('section', 'dp'))
- ffn1_in_grad: float32 [1024, 2, 4608], P(('section', 'dp'), None, 'tensor')
- ffn1_out_grad: float32 [4608, 1024], P('tensor', ('section', 'dp'))
- attn_qkv_grad: float32 [1024, 8, 256], P(('section', 'dp'), 'tensor')
- attn_out_grad: float32 [1024, 1024], P('tensor', ('section', 'dp'))
- ffn2_in_grad: float32 [1024, 2, 4608], P(('section', 'dp'), None, 'tensor')
- ffn2_out_grad: float32 [4608, 1024], P('tensor', ('section', 'dp'))
The draws below stay inside these ranges and needn't reach their ends.
Inputs may be any that keep to these rules, and one draw needn't show every extreme that they name: Each row holds the lengths of the 6 sequences packed one after another in a replica's stream; they sum to 4096, and the longest is exactly 1024.
All inputs are finite; a program needn't handle non-finite values.
Results may differ from the reference program's by a relative error of at most 0.025.
Values may be sent and summed in bfloat16 or wider, within the bound.
No kernel may reach another device: no remote copies, remote signals or barrier semaphores. Data moves between devices by JAX's collectives and lax.ppermute only.
A program may use at most 640 MiB of HBM per device.

```python
import math
import jax
import jax.numpy as jnp
import numpy as np
from jax import lax

D = 1024
FF = 4608
H = 16
KV = 8
HD = 64
SECTIONS = 4
MB = 4
TOK_MB = 1024
NSEQ = 6
STREAM = 4096
SEQ_MOST = 1024
ROWS = 2048
N_DP = 2


def shard_levels(own_key, shape, pieces, low, largest):
    def one(dim, shards_of):
        heights = jax.random.uniform(jax.random.fold_in(jax.random.fold_in(own_key, 6), dim), (shards_of,), jnp.float32, low / len(pieces), largest / len(pieces))
        return jnp.repeat(jnp.exp(heights), shape[dim] // shards_of).reshape((-1,) + (1,) * (len(shape) - dim - 1))

    factor_of = one(*pieces[0])
    for cut in pieces[1:]:
        factor_of = factor_of * one(*cut)
    return factor_of


def split_up(count, total, bound, skew):
    loads = [(1 << 20) // math.isqrt(rank ** skew) + 1 for rank in range(2, count + 1)]
    surplus, given = total - bound - (count - 1), [1] * (count - 1)
    while surplus > 0:
        candidates = [i for i in range(count - 1) if given[i] < bound]
        mass, left = sum([loads[i] for i in candidates]), surplus
        for i in candidates:
            extra = min(bound - given[i], max(1, left * loads[i] // mass), surplus)
            given[i] = given[i] + extra
            surplus = surplus - extra
    return np.array([bound] + given)


def ragged_sizes(stream_key, amount, total, bound, lean):
    if amount == 2:
        one = jax.random.randint(stream_key, (), max(1, total - bound), min(bound, total - 1) + 1)
        return jnp.stack([one, total - one])
    tallies = jnp.asarray(split_up(amount, total, bound, lean), jnp.int32)
    couples = (amount - 1) // 2
    donor, receiver = tallies[1:1 + 2 * couples:2], tallies[2:2 + 2 * couples:2]
    room = jnp.minimum(donor - 1, bound - receiver)
    moved = jax.random.randint(jax.random.fold_in(stream_key, 1), (couples,), 0, 1 << 20) % (room + 1)
    tallies = tallies.at[1:1 + 2 * couples:2].set(donor - moved).at[2:2 + 2 * couples:2].set(receiver + moved)
    return tallies[jax.random.permutation(jax.random.fold_in(stream_key, 2), amount)]


def bell_draw(stream_key, dims, width, reach, split=(), kind=jnp.bfloat16):
    values = width * jax.random.normal(stream_key, dims, jnp.float32)
    if split:
        values = values * shard_levels(stream_key, dims, split, -0.22, 0.18)
    return jnp.clip(values, -reach, reach).astype(kind)


def setup_inputs(seed: int = 0) -> dict:
    arg_keys = jax.random.split(jax.random.key(seed), 15)
    tokens = bell_draw(arg_keys[0], (MB, ROWS, D), 1.0, 6.0, ((0, 4), (1, 2), (2, 4)))
    lengths = jax.vmap(lambda own: ragged_sizes(own, NSEQ, STREAM, SEQ_MOST, 2))(jax.random.split(arg_keys[1], N_DP)).reshape((N_DP, NSEQ)).astype(jnp.int32)
    gains = jnp.clip(1.0 + 0.1 * jax.random.normal(arg_keys[2], (SECTIONS, D), jnp.float32), 0.5, 1.5)
    qk_gains = jnp.clip(1.0 + 0.1 * jax.random.normal(arg_keys[3], (2, HD), jnp.float32), 0.5, 1.5)
    conv_kernel = bell_draw(arg_keys[4], (3, D), 3 ** -0.5, 3.5, ((1, 4),))
    conv_in = bell_draw(arg_keys[5], (D, 3, D), D ** -0.5, 0.1875, ((0, 8), (2, 4)))
    conv_out = bell_draw(arg_keys[6], (D, D), D ** -0.5, 0.1875, ((0, 4), (1, 8)))
    ffn1_in = bell_draw(arg_keys[7], (D, 2, FF), D ** -0.5, 0.1875, ((0, 8), (2, 4)))
    ffn1_out = bell_draw(arg_keys[8], (FF, D), FF ** -0.5, 0.09375, ((0, 4), (1, 8)))
    attn_qkv = bell_draw(arg_keys[9], (D, KV, 4 * HD), D ** -0.5, 0.1875, ((0, 8), (1, 4)))
    attn_out = bell_draw(arg_keys[10], (H * HD, D), (max(H * HD // 256, 1)) ** -0.5, 3.0, ((0, 4), (1, 8)))
    ffn2_in = bell_draw(arg_keys[11], (D, 2, FF), D ** -0.5, 0.1875, ((0, 8), (2, 4)))
    ffn2_out = bell_draw(arg_keys[12], (FF, D), FF ** -0.5, 0.09375, ((0, 4), (1, 8)))
    cotangent = bell_draw(arg_keys[13], (MB, ROWS, D), 1.0, 6.0, ((0, 4), (1, 2), (2, 4)))
    return dict(tokens=tokens, lengths=lengths, gains=gains, qk_gains=qk_gains, conv_kernel=conv_kernel, conv_in=conv_in, conv_out=conv_out, ffn1_in=ffn1_in, ffn1_out=ffn1_out, attn_qkv=attn_qkv, attn_out=attn_out, ffn2_in=ffn2_in, ffn2_out=ffn2_out, cotangent=cotangent)


@jax.custom_vjp
def low(v):
    return lax.optimization_barrier(v.astype(jnp.bfloat16)).astype(jnp.float32)

@jax.custom_vjp
def low_back(v):
    return v

def low_keep(v):
    return (low(v), None)

def low_pass(kept, grad):
    return (grad,)

def back_keep(v):
    return (v, None)

def back_low(kept, grad):
    return (low(grad),)
low.defvjp(low_keep, low_pass)
low_back.defvjp(back_keep, back_low)
EPSILON = 1e-05
ROTARY_BASE = 1000000.0
NEGATIVE = -1e+30
HIGHEST = lax.Precision.HIGHEST

def rounded_both(values):
    return low_back(low(values))

def root_norm(values, gain_row):
    return values * lax.rsqrt(lax.optimization_barrier(jnp.mean(values * values, axis=-1, keepdims=True)) + EPSILON) * gain_row

def document_layout(sequence_lengths, total_rows):
    document_ends = jnp.cumsum(sequence_lengths).astype(jnp.int32)
    places = jnp.arange(total_rows, dtype=jnp.int32)
    passed = (places[:, None] >= document_ends[None, :]).astype(jnp.int32)
    documents = lax.optimization_barrier(jnp.sum(passed, axis=1)).astype(jnp.int32)
    offsets = (places - lax.optimization_barrier(jnp.sum(passed * sequence_lengths[None, :], axis=1))).astype(jnp.int32)
    return (documents, offsets)

def angles(offsets, head_width):
    inverse = ROTARY_BASE ** (-jnp.arange(0, head_width, 2).astype(jnp.float32) / head_width)
    phases = offsets.astype(jnp.float32)[:, None] * inverse[None, :]
    phases = jnp.concatenate([phases, phases], axis=1)
    return (jnp.cos(phases), jnp.sin(phases))

def rotary(values, cosine_rows, sine_rows):
    half_width = values.shape[-1] // 2
    turned = jnp.concatenate([-values[..., half_width:], values[..., :half_width]], axis=-1)
    return values * cosine_rows + turned * sine_rows

def convolve(product, tail_rows, offsets, kernel):
    extended = jnp.concatenate([tail_rows, product], axis=0)
    first_mask = (offsets >= 1).astype(product.dtype)[:, None]
    second_mask = (offsets >= 2).astype(product.dtype)[:, None]
    return kernel[2] * product + kernel[1] * extended[1:-1] * first_mask + kernel[0] * extended[:-2] * second_mask

def split_heads(packed, head_gains, cosine_rows, sine_rows):
    size_head = packed.shape[-1] // 4
    queries = packed[..., :2 * size_head].reshape(packed.shape[0], packed.shape[1], 2, size_head)
    key_heads = packed[..., 2 * size_head:3 * size_head]
    value_heads = packed[..., 3 * size_head:]
    queries = rotary(root_norm(queries, head_gains[0]), cosine_rows[:, None, None, :], sine_rows[:, None, None, :])
    key_heads = rotary(root_norm(key_heads, head_gains[1]), cosine_rows[:, None, :], sine_rows[:, None, :])
    return (queries, key_heads, value_heads)

def mixer_block(inputs, gain_row, inward, kernel, outward, offsets):
    normed = low(root_norm(inputs, gain_row))
    projected = low_back(jnp.einsum('td,dkc->tkc', normed, inward, precision=HIGHEST))
    product = projected[:, 0] * projected[:, 2]
    tail_rows = jnp.zeros((2, product.shape[1]), product.dtype)
    convolved = convolve(product, tail_rows, offsets, kernel)
    gated_values = low(projected[:, 1] * convolved)
    return jnp.dot(gated_values, outward, precision=HIGHEST)

def feed_forward(inputs, gain_row, inward, outward):
    normed = low(root_norm(inputs, gain_row))
    gate_up = low_back(jnp.einsum('td,dkf->tkf', normed, inward, precision=HIGHEST))
    hidden = low(jax.nn.silu(gate_up[:, 0]) * gate_up[:, 1])
    return jnp.dot(hidden, outward, precision=HIGHEST)

def attention(inputs, gain_row, head_gains, inward, outward, documents, offsets):
    total_rows = inputs.shape[0]
    normed = low(root_norm(inputs, gain_row))
    packed = low_back(jnp.einsum('td,dgc->tgc', normed, inward, precision=HIGHEST))
    cosine_rows, sine_rows = angles(offsets, HD)
    queries, key_heads, value_heads = split_heads(packed, head_gains, cosine_rows, sine_rows)
    queries = rounded_both(queries)
    key_heads = rounded_both(key_heads)
    value_heads = rounded_both(value_heads)
    block_rows = min(512, total_rows)
    places = jnp.arange(total_rows, dtype=jnp.int32)

    def attend_block(first_place):
        query_rows = lax.dynamic_slice_in_dim(queries, first_place, block_rows, 0)
        query_documents = lax.dynamic_slice_in_dim(documents, first_place, block_rows, 0)
        query_places = lax.dynamic_slice_in_dim(places, first_place, block_rows, 0)
        raw_scores = jnp.einsum('tgjd,sgd->gjts', query_rows, key_heads, precision=HIGHEST)
        scores = low_back(raw_scores * HD ** (-0.5))
        allowed = (documents[None, :] == query_documents[:, None]) & (places[None, :] <= query_places[:, None])
        scores = jnp.where(allowed, scores, NEGATIVE)
        row_max = lax.optimization_barrier(jnp.max(scores, axis=-1, keepdims=True))
        weights = jnp.exp(scores - row_max)
        weights = weights / lax.optimization_barrier(jnp.sum(weights, axis=-1, keepdims=True))
        attended = jnp.einsum('gjts,sgd->tgjd', low(weights), value_heads, precision=HIGHEST)
        return rounded_both(attended)
    starts = jnp.arange(0, total_rows, block_rows, dtype=jnp.int32)
    attended = lax.map(jax.checkpoint(attend_block), starts)
    return jnp.dot(attended.reshape(total_rows, H * HD), outward, precision=HIGHEST)

def stream_forward(stream, sequence_lengths, parameters):
    gains, head_gains, kernel, mixer_in, mixer_out, first_in, first_out, heads_in, heads_out, second_in, second_out = parameters
    documents, offsets = document_layout(sequence_lengths, stream.shape[0])
    residual = rounded_both(stream + mixer_block(stream, gains[0], mixer_in, kernel, mixer_out, offsets))
    residual = rounded_both(residual + feed_forward(residual, gains[1], first_in, first_out))
    residual = rounded_both(residual + attention(residual, gains[2], head_gains, heads_in, heads_out, documents, offsets))
    return low(residual + feed_forward(residual, gains[3], second_in, second_out))

def reference(tokens, lengths, gains, qk_gains, conv_kernel, conv_in, conv_out, ffn1_in, ffn1_out, attn_qkv, attn_out, ffn2_in, ffn2_out, cotangent):
    parameters = tuple((weight_array.astype(jnp.float32) for weight_array in (gains, qk_gains, conv_kernel, conv_in, conv_out, ffn1_in, ffn1_out, attn_qkv, attn_out, ffn2_in, ffn2_out)))

    def forward(token_values, weight_set):
        streams = token_values.reshape(MB, N_DP, TOK_MB, D).transpose(1, 0, 2, 3).reshape(N_DP, MB * TOK_MB, D)

        def replica_turn(unused_carry, replica_item):
            return (unused_carry, jax.checkpoint(stream_forward)(replica_item[0], replica_item[1], weight_set))
        _, finished = lax.scan(replica_turn, jnp.zeros((), jnp.float32), (streams, lengths))
        return finished.reshape(N_DP, MB, TOK_MB, D).transpose(1, 0, 2, 3).reshape(MB, N_DP * TOK_MB, D)
    output, pull_back = jax.vjp(forward, tokens.astype(jnp.float32), parameters)
    input_grad, weight_grads = pull_back(cotangent.astype(jnp.float32))
    return (output.astype(jnp.bfloat16), input_grad.astype(jnp.bfloat16), weight_grads[0], weight_grads[1], weight_grads[2], weight_grads[3], weight_grads[4], weight_grads[5], weight_grads[6], weight_grads[7], weight_grads[8], weight_grads[9], weight_grads[10])
```

```python
import functools

import jax
import jax.numpy as jnp
from jax import lax
from jax.experimental import pallas as pl
from jax.experimental.pallas import tpu as pltpu
from jax.sharding import PartitionSpec as P

EPSILON = 1e-05
ROTARY_BASE = 1000000.0
NEGATIVE = -1e30
AXES = ("section", "tensor", "dp")
LOW = jnp.bfloat16
WIDE = jnp.float32
RANKS = 4
LONGEST = 1024


class Place:
    def __init__(self):
        self.sections = lax.axis_size("section")
        self.depth = lax.axis_size("tensor")
        self.replicas = lax.axis_size("dp")
        self.rings = self.replicas // 2
        section = lax.axis_index("section")
        self.z = lax.axis_index("tensor")
        replica = lax.axis_index("dp")
        self.half, self.side = section // 2, section % 2
        self.ring, self.core = replica // 2, replica % 2
        self.rank = 2 * self.side + self.core

    def move(self, values, target):
        route = []
        for half in range(self.sections // 2):
            for side in range(2):
                for z in range(self.depth):
                    for ring in range(self.rings):
                        for core in range(2):
                            goal = target(half, side, z, ring, core)
                            if goal is not None:
                                route.append(
                                    (self.flat(half, side, z, ring, core), self.flat(*goal))
                                )
        return lax.ppermute(values, AXES, route)

    def flat(self, half, side, z, ring, core):
        return ((half * 2 + side) * self.depth + z) * self.replicas + ring * 2 + core

    def to_rank(self, values, k):
        return self.move(
            values, lambda half, side, z, ring, core: (half, side ^ (k >> 1), z, ring, core ^ (k & 1))
        )

    def to_half(self, values):
        return self.move(
            values, lambda half, side, z, ring, core: (1 - half, side, z, ring, core)
        )

    def up(self, values, distance=1):
        return self.move(
            values,
            lambda half, side, z, ring, core: (half, side, z + distance, ring, core)
            if 0 <= z + distance < self.depth
            else None,
        )

    def to_ring(self, values, distance):
        return self.move(
            values,
            lambda half, side, z, ring, core: (half, side, z, (ring + distance) % self.rings, core),
        )

    def across_z(self, values, bit):
        return self.move(
            values, lambda half, side, z, ring, core: (half, side, z ^ bit, ring, core)
        )

    def across_ring(self, values, bit):
        return self.move(
            values, lambda half, side, z, ring, core: (half, side, z, ring ^ bit, core)
        )

    def turn(self, values):
        width = values.shape[-1] // 2
        turned = jnp.concatenate([values[..., width:], values[..., :width]], axis=-1)
        return jnp.where(self.half == 0, values, turned)

    def by_rank(self, blocks):
        return [
            lax.select_n(jnp.bitwise_xor(self.rank, b), *blocks) for b in range(RANKS)
        ]

    def mirrored(self, stacked, place):
        count = stacked.shape[0]
        flipped = jnp.concatenate([stacked[:1], stacked[:0:-1]], axis=0)
        return lax.dynamic_slice_in_dim(
            jnp.concatenate([flipped, flipped], axis=0), count - place, count, 0
        )

    def rolled(self, stacked, place):
        count = stacked.shape[0]
        return lax.dynamic_slice_in_dim(
            jnp.concatenate([stacked, stacked], axis=0), count - place, count, 0
        )

    def gather_z(self, values):
        upward, downward = [values], [values]
        for _ in range(self.depth - 1):
            upward.append(self.up(upward[-1], 1))
            downward.append(self.up(downward[-1], -1))
        return [values] + [
            upward[s] + downward[self.depth - s] for s in range(1, self.depth)
        ]

    def scatter_z(self, parts):
        upward = downward = None
        for t in range(1, self.depth):
            rest = self.depth - t
            ahead = jnp.where(self.z < t, parts[t], 0).astype(LOW)
            behind = jnp.where(self.z >= rest, parts[rest], 0).astype(LOW)
            if upward is not None:
                ahead = (ahead.astype(WIDE) + upward.astype(WIDE)).astype(LOW)
                behind = (behind.astype(WIDE) + downward.astype(WIDE)).astype(LOW)
            upward, downward = self.up(ahead, 1), self.up(behind, -1)
        return (parts[0].astype(WIDE) + upward.astype(WIDE) + downward.astype(WIDE)).astype(LOW)

    def gather_half(self, values):
        return jnp.concatenate([values, self.to_half(values)], axis=-1)

    def scatter_half(self, values):
        width = values.shape[-1] // 2
        other = self.to_half(values[..., width:].astype(LOW))
        return (values[..., :width].astype(WIDE) + other.astype(WIDE)).astype(LOW)

    def exchange(self, parts):
        if self.rings > 1:
            found = [parts] + [self.to_ring(parts, k) for k in range(1, self.rings)]
            parts = self.mirrored(jnp.stack(found), self.ring)
        else:
            parts = parts[None]
        blocks = []
        for k in range(RANKS):
            part = lax.dynamic_index_in_dim(
                parts, jnp.bitwise_xor(self.rank, k), 1, keepdims=False
            )
            blocks.append(part if k == 0 else self.to_rank(part, k))
        blocks = self.by_rank(blocks)
        ordered = [
            blocks[2 * side + core][ring]
            for side in range(2)
            for ring in range(self.rings)
            for core in range(2)
        ]
        return jnp.concatenate(ordered, axis=-1)

    def exchange_back(self, values):
        block = values.shape[-1] // (RANKS * self.rings)
        grid = values.reshape(values.shape[0], 2, self.rings, 2, block)
        stacked = jnp.stack(
            [grid[:, side, :, core] for side in range(2) for core in range(2)]
        ).transpose(0, 2, 1, 3)
        blocks = []
        for k in range(RANKS):
            part = lax.dynamic_index_in_dim(
                stacked, jnp.bitwise_xor(self.rank, k), 0, keepdims=False
            )
            blocks.append(part if k == 0 else self.to_rank(part, k))
        parts = jnp.stack(self.by_rank(blocks), axis=1)
        if self.rings == 1:
            return parts[0]
        total = lax.dynamic_index_in_dim(parts, self.ring, 0, keepdims=False).astype(WIDE)
        for k in range(1, self.rings):
            sent = lax.dynamic_index_in_dim(
                parts, (self.ring + k) % self.rings, 0, keepdims=False
            )
            total = total + self.to_ring(sent, k).astype(WIDE)
        return total

    def gather_rows(self, values):
        mate = self.to_rank(values, 1)
        across = self.to_rank(values, 2)
        return [values, mate, across, self.to_rank(across, 1)]

    def scatter_rows(self, blocks):
        rows = blocks[0].shape[0]
        came = self.to_rank(jnp.concatenate([blocks[1], blocks[3]], axis=0).astype(LOW), 1)
        across = (blocks[2].astype(WIDE) + came[rows:].astype(WIDE)).astype(LOW)
        own = blocks[0].astype(WIDE) + came[:rows].astype(WIDE)
        return own + self.to_rank(across, 2).astype(WIDE)

    def total(self, values):
        for k in (1, 2):
            values = values + self.to_rank(values, k)
        values = values + self.to_half(values)
        bit = 1
        while bit < self.depth:
            values = values + self.across_z(values, bit)
            bit *= 2
        bit = 1
        while bit < self.rings:
            values = values + self.across_ring(values, bit)
            bit *= 2
        return values


def times(a, b):
    return lax.dot_general(a, b, (((1,), (0,)), ((), ())), preferred_element_type=WIDE)


def times_rows(a, b):
    return lax.dot_general(a, b, (((1,), (1,)), ((), ())), preferred_element_type=WIDE)


def columns_times(a, b):
    return lax.dot_general(a, b, (((0,), (0,)), ((), ())), preferred_element_type=WIDE)


def root_norm(values, gain_row):
    return (
        values * lax.rsqrt(jnp.mean(values * values, axis=-1, keepdims=True) + EPSILON) * gain_row
    )


def root_norm_back(inputs, gain_row, grad, arriving):
    widened = inputs.astype(WIDE)
    inverse = lax.rsqrt(jnp.mean(widened * widened, axis=-1, keepdims=True) + EPSILON)
    unit_rows = widened * inverse
    scaled = grad * gain_row
    through = inverse * (scaled - unit_rows * jnp.mean(scaled * unit_rows, axis=-1, keepdims=True))
    gain_grad = jnp.sum(grad * unit_rows, axis=0)
    return ((arriving.astype(WIDE) + through).astype(LOW), gain_grad)


def angles(offsets, head_width):
    inverse = ROTARY_BASE ** (-jnp.arange(0, head_width, 2).astype(WIDE) / head_width)
    phases = offsets.astype(WIDE)[:, None] * inverse[None, :]
    phases = jnp.concatenate([phases, phases], axis=1)
    return (jnp.cos(phases), jnp.sin(phases))


def rotary(values, cosine_rows, sine_rows):
    half_width = values.shape[-1] // 2
    turned = jnp.concatenate([-values[..., half_width:], values[..., :half_width]], axis=-1)
    return values * cosine_rows + turned * sine_rows


def split_heads(packed, head_gains, cosine_rows, sine_rows):
    size_head = packed.shape[-1] // 4
    queries = packed[..., : 2 * size_head].reshape(packed.shape[0], packed.shape[1], 2, size_head)
    key_heads = packed[..., 2 * size_head : 3 * size_head]
    value_heads = packed[..., 3 * size_head :]
    queries = rotary(
        root_norm(queries, head_gains[0]),
        cosine_rows[:, None, None, :],
        sine_rows[:, None, None, :],
    )
    key_heads = rotary(
        root_norm(key_heads, head_gains[1]), cosine_rows[:, None, :], sine_rows[:, None, :]
    )
    return (queries, key_heads, value_heads)


def block_weights(offsets, queries, keys, scale):
    scores = (
        lax.dot_general(queries, keys, (((1,), (1,)), ((), ())), preferred_element_type=WIDE)
        * scale
    )
    rows, window = offsets.shape[0], keys.shape[0]
    shape = (rows, window)
    back = (
        lax.broadcasted_iota(jnp.int32, shape, 0)
        + LONGEST
        - lax.broadcasted_iota(jnp.int32, shape, 1)
    )
    allowed = (back >= 0) & (back <= offsets)
    allowed = jnp.concatenate([allowed.astype(WIDE)] * (queries.shape[0] // rows), axis=0) > 0.5
    scores = jnp.where(allowed, scores, NEGATIVE)
    weights = jnp.exp(scores - jnp.max(scores, axis=-1, keepdims=True))
    return weights / jnp.sum(weights, axis=-1, keepdims=True)


def attend_kernel(scale, offsets_ref, queries_ref, keys_ref, values_ref, out_ref):
    rows, width = queries_ref.shape[2], queries_ref.shape[3]
    low = pl.multiple_of(pl.program_id(1) * rows, rows)
    window = pl.ds(low, LONGEST + rows)
    queries = queries_ref[0].reshape(2 * rows, width)
    weights = block_weights(offsets_ref[...], queries, keys_ref[0, window, :], scale)
    result = jnp.dot(
        weights.astype(LOW), values_ref[0, window, :], preferred_element_type=WIDE
    ).astype(LOW)
    out_ref[0] = result.reshape(2, rows, width)


def attend_back_kernel(
    scale,
    offsets_ref,
    queries_ref,
    keys_ref,
    values_ref,
    grad_ref,
    queries_grad_ref,
    keys_grad_ref,
    values_grad_ref,
):
    rows, width = queries_ref.shape[2], queries_ref.shape[3]

    @pl.when(pl.program_id(1) == 0)
    def _():
        keys_grad_ref[...] = jnp.zeros_like(keys_grad_ref)
        values_grad_ref[...] = jnp.zeros_like(values_grad_ref)

    low = pl.multiple_of(pl.program_id(1) * rows, rows)
    window = pl.ds(low, LONGEST + rows)
    queries = queries_ref[0].reshape(2 * rows, width)
    grad = grad_ref[0].reshape(2 * rows, width)
    keys, values = keys_ref[0, window, :], values_ref[0, window, :]
    weights = block_weights(offsets_ref[...], queries, keys, scale)
    flow = lax.dot_general(grad, values, (((1,), (1,)), ((), ())), preferred_element_type=WIDE)
    inner = jnp.sum(weights * flow, axis=-1, keepdims=True)
    score_grad = (weights * (flow - inner)).astype(LOW)
    values_grad_ref[0, window, :] += lax.dot_general(
        weights.astype(LOW), grad, (((0,), (0,)), ((), ())), preferred_element_type=WIDE
    )
    keys_grad_ref[0, window, :] += (
        lax.dot_general(
            score_grad, queries, (((0,), (0,)), ((), ())), preferred_element_type=WIDE
        )
        * scale
    )
    queries_grad = jnp.dot(score_grad, keys, preferred_element_type=WIDE) * scale
    queries_grad_ref[0] = queries_grad.astype(LOW).reshape(2, rows, width)


def attention_specs(queries, keys, rows):
    groups, _, total, width = queries.shape
    grid = (groups, total // rows)
    offsets_spec = pl.BlockSpec((rows, 1), lambda g, i: (i, 0))
    rows_spec = pl.BlockSpec((1, 2, rows, width), lambda g, i: (g, 0, i, 0))
    keys_spec = pl.BlockSpec((1, keys.shape[1], width), lambda g, i: (g, 0, 0))
    return (grid, offsets_spec, rows_spec, keys_spec)


def attend(offsets, queries, keys, values, rows):
    grid, offsets_spec, rows_spec, keys_spec = attention_specs(queries, keys, rows)
    return pl.pallas_call(
        functools.partial(attend_kernel, queries.shape[-1] ** (-0.5)),
        grid=grid,
        in_specs=[offsets_spec, rows_spec, keys_spec, keys_spec],
        out_specs=rows_spec,
        out_shape=jax.ShapeDtypeStruct(queries.shape, LOW),
        compiler_params=pltpu.CompilerParams(vmem_limit_bytes=48 << 20),
        name="attend",
    )(offsets[:, None], queries, keys, values)


def attend_back(offsets, queries, keys, values, grad, rows):
    grid, offsets_spec, rows_spec, keys_spec = attention_specs(queries, keys, rows)
    return pl.pallas_call(
        functools.partial(attend_back_kernel, queries.shape[-1] ** (-0.5)),
        grid=grid,
        in_specs=[offsets_spec, rows_spec, keys_spec, keys_spec, rows_spec],
        out_specs=[rows_spec, keys_spec, keys_spec],
        out_shape=[
            jax.ShapeDtypeStruct(queries.shape, LOW),
            jax.ShapeDtypeStruct(keys.shape, WIDE),
            jax.ShapeDtypeStruct(keys.shape, WIDE),
        ],
        compiler_params=pltpu.CompilerParams(vmem_limit_bytes=48 << 20),
        name="attend_back",
    )(offsets[:, None], queries, keys, values, grad)


def local(
    tokens,
    lengths,
    gains,
    qk_gains,
    conv_kernel,
    conv_in,
    conv_out,
    ffn1_in,
    ffn1_out,
    attn_qkv,
    attn_out,
    ffn2_in,
    ffn2_out,
    cotangent,
):
    here = Place()
    depth = here.depth
    stretch = tokens.shape[1]
    slice_width = tokens.shape[2]
    model_width = slice_width * depth
    stream_rows = here.sections * stretch
    team_rows = stream_rows // depth
    own_rows = team_rows // RANKS
    head_width = attn_qkv.shape[2] // 4
    groups_here = attn_qkv.shape[1]
    groups = groups_here * depth // RANKS
    block_width = conv_in.shape[0]
    query_rows = min(256, team_rows)

    teams = depth // here.sections

    def row_goal(k):
        def goal(half, side, z, ring, core):
            part = (z + k) % depth
            rank = part % RANKS
            batch = half * 2 + side
            return (core, rank // 2, batch * (depth // RANKS) + part // RANKS, ring, rank % 2)

        return goal

    def flat_goal(k):
        return {
            here.flat(*source): here.flat(*row_goal(k)(*source))
            for source in (
                (half, side, z, ring, core)
                for half in range(here.sections // 2)
                for side in range(2)
                for z in range(depth)
                for ring in range(here.rings)
                for core in range(2)
            )
        }

    own_part = (here.z % (depth // RANKS)) * RANKS + here.rank

    def rows_in(values):
        grid = values[0].reshape(depth, own_rows, slice_width)
        pieces = []
        for k in range(depth):
            piece = lax.dynamic_index_in_dim(grid, (here.z + k) % depth, 0, keepdims=False)
            pieces.append(lax.ppermute(piece, AXES, sorted(flat_goal(k).items())))
        columns = here.mirrored(jnp.stack(pieces), own_part)
        return here.turn(columns.transpose(1, 0, 2).reshape(own_rows, model_width))

    def rows_out(values):
        grid = here.turn(values).reshape(own_rows, depth, slice_width)
        pieces = []
        for k in range(depth):
            piece = lax.dynamic_index_in_dim(
                grid, (own_part - k) % depth, 1, keepdims=False
            )
            route = sorted((goal, source) for source, goal in flat_goal(k).items())
            pieces.append(lax.ppermute(piece, AXES, route))
        return here.rolled(jnp.stack(pieces), here.z).reshape(1, stretch, slice_width)

    def by_ranks(values):
        kinds, rows, columns = values.shape
        share = rows // RANKS
        return (
            values.reshape(kinds, RANKS, share, columns)
            .transpose(1, 0, 2, 3)
            .reshape(RANKS, kinds * share, columns)
        )

    def from_ranks(values, kinds):
        _, rows, columns = values.shape
        share = rows // kinds
        return (
            values.reshape(RANKS, kinds, share, columns)
            .transpose(1, 0, 2, 3)
            .reshape(kinds, RANKS * share, columns)
        )

    def slots_together(slots, kinds):
        rows, columns = slots[0].shape
        return jnp.stack(
            [slot.reshape(kinds, rows // kinds, columns) for slot in slots], axis=1
        ).reshape(kinds * depth * (rows // kinds), columns)

    def slots_apart(values, kinds):
        rows, columns = values.shape
        grid = values.reshape(kinds, depth, rows // (kinds * depth), columns)
        return [grid[:, s].reshape(rows // depth, columns) for s in range(depth)]

    def inward(values):
        return values.transpose(1, 2, 0)

    def gather_z_first(values, kinds):
        slots = here.gather_z(here.exchange(by_ranks(values)))
        return slots_together([here.gather_half(slot) for slot in slots], kinds)

    def scatter_half_first(grad, kinds):
        parts = [here.scatter_half(part) for part in slots_apart(grad.astype(LOW), kinds)]
        return from_ranks(here.exchange_back(here.scatter_z(parts)), kinds)

    taps = conv_kernel.shape[0]
    share = slice_width // RANKS
    mixer_parts = here.exchange(
        by_ranks(jnp.concatenate([inward(conv_in), conv_out[None]], axis=0))
    )
    own_taps = lax.dynamic_slice_in_dim(conv_kernel, here.rank * share, share, 1)
    own_taps = jnp.pad(own_taps, ((0, 16 - taps), (0, mixer_parts.shape[1] - share)))
    mixer_slots = here.gather_z(
        here.gather_half(jnp.concatenate([mixer_parts, own_taps], axis=0))
    )
    mixer_weights = slots_together([slot[: 4 * share] for slot in mixer_slots], 4)
    channels = depth * share
    mixer_inward, mixer_outward = mixer_weights[: 3 * channels], mixer_weights[3 * channels :]
    kernel = jnp.concatenate(
        [slot[4 * share : 4 * share + taps, :share] for slot in mixer_slots], axis=1
    ).astype(WIDE)

    first_inward = gather_z_first(inward(ffn1_in), 2)
    first_outward = gather_z_first(ffn1_out[None], 1)

    heads_rows = attn_out.shape[0] // groups_here
    heads_parts = jnp.concatenate(
        [inward(attn_qkv), attn_out.reshape(groups_here, heads_rows, -1)], axis=1
    )
    heads_size = heads_parts.shape[1]
    heads_parts = here.mirrored(jnp.stack(here.gather_z(heads_parts)), here.z)
    heads_weights = here.gather_half(
        here.exchange(heads_parts.reshape(RANKS, groups * heads_size, block_width))
    ).reshape(groups, heads_size, model_width)
    heads_inward = heads_weights[:, : heads_size - heads_rows].reshape(-1, model_width)
    heads_outward = heads_weights[:, heads_size - heads_rows :].reshape(-1, model_width)

    second_inward = gather_z_first(inward(ffn2_in), 2)
    second_outward = gather_z_first(ffn2_out[None], 1)

    own_lengths = jnp.where(here.half == here.core, lengths[0], here.to_rank(lengths[0], 1))
    places = here.z * team_rows + jnp.arange(team_rows + 2, dtype=jnp.int32)
    passed = (places[:, None] >= jnp.cumsum(own_lengths)[None, :]).astype(jnp.int32)
    offsets = places - jnp.sum(passed * own_lengths[None, :], axis=1)
    first_mask = (offsets >= 1).astype(WIDE)[:, None]
    second_mask = (offsets >= 2).astype(WIDE)[:, None]
    offsets = offsets[:team_rows]
    cosine_rows, sine_rows = angles(offsets, head_width)
    all_gains = here.turn(lax.all_gather(gains, "section", axis=0, tiled=True))

    def gather_ordered(values):
        return jnp.concatenate(here.by_rank(here.gather_rows(values)), axis=0)

    def gather_any(values):
        return jnp.concatenate(here.gather_rows(values), axis=0)

    def scatter_ordered(values):
        grid = values.astype(LOW).reshape(RANKS, own_rows, model_width)
        return here.scatter_rows(
            [
                lax.dynamic_index_in_dim(
                    grid, jnp.bitwise_xor(here.rank, k), 0, keepdims=False
                )
                for k in range(RANKS)
            ]
        )

    def scatter_any(values):
        grid = values.astype(LOW).reshape(RANKS, own_rows, model_width)
        return here.scatter_rows([grid[k] for k in range(RANKS)])

    def joined(residual, update):
        return (residual.astype(WIDE) + update).astype(LOW)

    def neighbour_rows(values, distance):
        moved = here.up(values, distance)
        return jnp.roll(
            moved.reshape(values.shape[0], depth, share), distance, axis=1
        ).reshape(values.shape)

    def mixer_forward(residual):
        normed = gather_ordered(root_norm(residual.astype(WIDE), all_gains[0]).astype(LOW))
        projected = times_rows(normed, mixer_inward)
        before, gate, after = (
            projected[:, :channels],
            projected[:, channels : 2 * channels],
            projected[:, 2 * channels :],
        )
        product = before * after
        tail = neighbour_rows(product[-2:], 1)
        extended = jnp.concatenate([tail, product], axis=0)
        once = extended[1:-1] * first_mask[:team_rows]
        twice = extended[:-2] * second_mask[:team_rows]
        mixed = kernel[2] * product + kernel[1] * once + kernel[0] * twice
        gated = (gate * mixed).astype(LOW)
        update = scatter_ordered(times(gated, mixer_outward))
        return joined(residual, update), (
            residual, normed, before, gate, after, product, once, twice, mixed, gated,
        )

    def mixer_backward(arriving, saved):
        residual, normed, before, gate, after, product, once, twice, mixed, gated = saved
        full = gather_ordered(arriving)
        gated_grad = times_rows(full, mixer_outward)
        outward_grad = columns_times(gated, full)
        gate_grad = gated_grad * mixed
        mixed_grad = gated_grad * gate
        extended = jnp.concatenate([mixed_grad, neighbour_rows(mixed_grad[:2], -1)], axis=0)
        product_grad = (
            kernel[2] * mixed_grad
            + kernel[1] * extended[1:-1] * first_mask[1:-1]
            + kernel[0] * extended[2:] * second_mask[2:]
        )
        kernel_grad = jnp.stack(
            [
                jnp.sum(mixed_grad * twice, axis=0),
                jnp.sum(mixed_grad * once, axis=0),
                jnp.sum(mixed_grad * product, axis=0),
            ]
        )
        low = jnp.concatenate(
            [product_grad * after, gate_grad, product_grad * before], axis=1
        ).astype(LOW)
        update = scatter_ordered(times(low, mixer_inward))
        grad = jnp.concatenate([columns_times(low, normed), outward_grad], axis=0)
        leaving, gain_grad = root_norm_back(residual, all_gains[0], update, arriving)
        return leaving, gain_grad, kernel_grad, grad

    def feed_forward(residual, gain_row, inward_weights, outward_weights):
        normed = gather_any(root_norm(residual.astype(WIDE), gain_row).astype(LOW))
        gate_up = times_rows(normed, inward_weights)
        width = gate_up.shape[1] // 2
        hidden = (jax.nn.silu(gate_up[:, :width]) * gate_up[:, width:]).astype(LOW)
        update = scatter_any(times(hidden, outward_weights))
        return joined(residual, update), (residual, normed, gate_up, hidden)

    def feed_backward(arriving, saved, gain_row, inward_weights, outward_weights):
        residual, normed, gate_up, hidden = saved
        full = gather_any(arriving)
        outward_grad = columns_times(hidden, full)
        hidden_grad = times_rows(full, outward_weights)
        width = gate_up.shape[1] // 2
        gate, up = gate_up[:, :width], gate_up[:, width:]
        sigmoid = jax.nn.sigmoid(gate)
        low = jnp.concatenate(
            [
                hidden_grad * up * (sigmoid * (1 + gate * (1 - sigmoid))),
                hidden_grad * (gate * sigmoid),
            ],
            axis=1,
        ).astype(LOW)
        update = scatter_any(times(low, inward_weights))
        inward_grad = columns_times(low, normed)
        leaving, gain_grad = root_norm_back(residual, gain_row, update, arriving)
        return leaving, gain_grad, inward_grad, outward_grad

    halo_steps = LONGEST // team_rows

    def heads_forward(residual):
        normed = gather_ordered(root_norm(residual.astype(WIDE), all_gains[2]).astype(LOW))
        packed = times_rows(normed, heads_inward).reshape(team_rows, groups, 4 * head_width)
        queries, keys, values = split_heads(packed, qk_gains, cosine_rows, sine_rows)
        queries = queries.astype(LOW).transpose(1, 2, 0, 3)
        pairs = jnp.stack([keys, values]).astype(LOW).transpose(0, 2, 1, 3)
        window = jnp.concatenate(
            [here.up(pairs, step) for step in range(halo_steps, 0, -1)] + [pairs], axis=2
        )
        attended = attend(offsets, queries, window[0], window[1], query_rows)
        flat = attended.transpose(2, 0, 1, 3).reshape(team_rows, -1)
        update = scatter_ordered(times(flat, heads_outward))
        return joined(residual, update), (residual, normed, packed, queries, window, flat)

    def heads_backward(arriving, saved):
        residual, normed, packed, queries, window, flat = saved
        full = gather_ordered(arriving)
        outward_grad = columns_times(flat, full)
        attended_grad = (
            times_rows(full, heads_outward)
            .astype(LOW)
            .reshape(team_rows, groups, 2, head_width)
            .transpose(1, 2, 0, 3)
        )
        queries_grad, keys_grad, values_grad = attend_back(
            offsets, queries, window[0], window[1], attended_grad, query_rows
        )
        flow = jnp.stack([keys_grad, values_grad])
        own = flow[:, :, LONGEST:]
        for step in range(1, halo_steps + 1):
            low = (halo_steps - step) * team_rows
            own = own + here.up(flow[:, :, low : low + team_rows].astype(LOW), -step).astype(WIDE)
        own = own.astype(LOW).astype(WIDE).transpose(0, 2, 1, 3)
        _, pull_heads = jax.vjp(
            lambda values, scales: split_heads(values, scales, cosine_rows, sine_rows),
            packed,
            qk_gains,
        )
        packed_grad, head_gains_grad = pull_heads(
            (queries_grad.astype(WIDE).transpose(2, 0, 1, 3), own[0], own[1])
        )
        low = packed_grad.astype(LOW).reshape(team_rows, -1)
        update = scatter_ordered(times(low, heads_inward))
        inward_grad = columns_times(low, normed)
        grad = jnp.concatenate(
            [
                inward_grad.reshape(groups, -1, model_width),
                outward_grad.reshape(groups, -1, model_width),
            ],
            axis=1,
        )
        leaving, gain_grad = root_norm_back(residual, all_gains[2], update, arriving)
        return leaving, gain_grad, head_gains_grad, grad

    residual = rows_in(tokens)
    residual, mixer_saved = mixer_forward(residual)
    residual, first_saved = feed_forward(residual, all_gains[1], first_inward, first_outward)
    residual, heads_saved = heads_forward(residual)
    residual, second_saved = feed_forward(residual, all_gains[3], second_inward, second_outward)
    output = rows_out(residual)

    flowing = rows_in(cotangent)
    flowing, gain3, second_inward_grad, second_outward_grad = feed_backward(
        flowing, second_saved, all_gains[3], second_inward, second_outward
    )
    flowing, gain2, head_gains_grad, heads_grad = heads_backward(flowing, heads_saved)
    flowing, gain1, first_inward_grad, first_outward_grad = feed_backward(
        flowing, first_saved, all_gains[1], first_inward, first_outward
    )
    flowing, gain0, kernel_grad, mixer_grad = mixer_backward(flowing, mixer_saved)
    input_grad = rows_out(flowing)

    second_outward_grad = scatter_half_first(second_outward_grad, 1)[0]
    second_inward_grad = scatter_half_first(second_inward_grad, 2)
    heads_grad = here.exchange_back(
        here.scatter_half(heads_grad.reshape(-1, model_width).astype(LOW))
    ).astype(LOW)
    heads_grad = heads_grad.reshape(depth, groups_here * heads_size, block_width)
    heads_grad = here.mirrored(heads_grad, here.z)
    heads_grad = here.scatter_z([heads_grad[s] for s in range(depth)])
    heads_grad = heads_grad.reshape(groups_here, heads_size, block_width)
    first_outward_grad = scatter_half_first(first_outward_grad, 1)[0]
    first_inward_grad = scatter_half_first(first_inward_grad, 2)
    mixer_grad = from_ranks(
        here.exchange_back(
            here.scatter_half(here.scatter_z(slots_apart(mixer_grad.astype(LOW), 4)))
        ),
        4,
    )

    def outside(values):
        return values.transpose(2, 0, 1).astype(WIDE)

    kernel_slots = kernel_grad.reshape(taps, depth, share).transpose(1, 0, 2)
    kernel_blocks = here.mirrored(kernel_slots, here.z).transpose(1, 0, 2)
    chosen = (jnp.arange(RANKS) == here.rank).astype(WIDE)
    kernel_whole = (kernel_blocks[:, :, None, :] * chosen[None, None, :, None]).reshape(
        taps, model_width
    )
    small = jnp.concatenate(
        [
            here.turn(jnp.stack([gain0, gain1, gain2, gain3])).reshape(-1),
            kernel_whole.reshape(-1),
            head_gains_grad.reshape(-1),
        ]
    )
    small = here.total(small)
    gain_size, kernel_size = 4 * model_width, taps * model_width
    return (
        output,
        input_grad,
        small[:gain_size].reshape(4, model_width),
        small[gain_size + kernel_size :].reshape(2, head_width),
        small[gain_size : gain_size + kernel_size].reshape(taps, model_width),
        outside(mixer_grad[:3]),
        mixer_grad[3].astype(WIDE),
        outside(first_inward_grad),
        first_outward_grad.astype(WIDE),
        outside(heads_grad[:, : heads_size - heads_rows]),
        heads_grad[:, heads_size - heads_rows :].reshape(attn_out.shape).astype(WIDE),
        outside(second_inward_grad),
        second_outward_grad.astype(WIDE),
    )


def solution(mesh):
    rows = P(("section", "dp"), None, "tensor")
    columns = P("tensor", ("section", "dp"))
    heads = P(("section", "dp"), "tensor", None)
    stream = P("section", "dp", "tensor")
    return jax.shard_map(
        local,
        mesh=mesh,
        in_specs=(
            stream,
            P("dp", None),
            P("section", None),
            P(),
            P(None, "tensor"),
            rows,
            columns,
            rows,
            columns,
            heads,
            columns,
            rows,
            columns,
            stream,
        ),
        out_specs=(
            stream,
            stream,
            P(),
            P(),
            P(),
            rows,
            columns,
            rows,
            columns,
            heads,
            columns,
            rows,
            columns,
        ),
        check_vma=False,
    )
```

```python
import functools

import jax
import jax.numpy as jnp
from jax import lax
from jax.experimental import pallas as pl
from jax.experimental.pallas import tpu as pltpu
from jax.sharding import Mesh
from jax.sharding import PartitionSpec as P

EPSILON = 1e-05
ROTARY_BASE = 1000000.0
NEGATIVE = -1e30
AXES = ("half", "side", "depth", "ring", "core")
SQUARE = ("half", "side", "ring", "core")
LOW = jnp.bfloat16
WIDE = jnp.float32
RANKS = 4
LONGEST = 1024


class Place:
    def __init__(self):
        self.halves = lax.axis_size("half")
        self.depth = lax.axis_size("depth")
        self.rings = lax.axis_size("ring")
        self.half = lax.axis_index("half")
        self.side = lax.axis_index("side")
        self.z = lax.axis_index("depth")
        self.ring = lax.axis_index("ring")
        self.core = lax.axis_index("core")
        self.rank = 2 * self.side + self.core

    def places(self):
        return [
            (half, side, z, ring, core)
            for half in range(self.halves)
            for side in range(2)
            for z in range(self.depth)
            for ring in range(self.rings)
            for core in range(2)
        ]

    def flat(self, half, side, z, ring, core):
        return (((half * 2 + side) * self.depth + z) * self.rings + ring) * 2 + core

    def route(self, target):
        pairs = [(place, target(*place)) for place in self.places()]
        return [(self.flat(*a), self.flat(*b)) for a, b in pairs if b is not None]

    def move(self, values, target):
        return lax.ppermute(values, AXES, self.route(target))

    def to_rank(self, values, k):
        return self.move(
            values, lambda half, side, z, ring, core: (half, side ^ (k >> 1), z, ring, core ^ (k & 1))
        )

    def up(self, values, distance=1):
        return self.move(
            values,
            lambda half, side, z, ring, core: (half, side, z + distance, ring, core)
            if 0 <= z + distance < self.depth
            else None,
        )

    def by_rank(self, blocks):
        return [
            lax.select_n(jnp.bitwise_xor(self.rank, b), *blocks) for b in range(RANKS)
        ]

    def mirrored(self, stacked, place):
        count = stacked.shape[0]
        flipped = jnp.concatenate([stacked[:1], stacked[:0:-1]], axis=0)
        return lax.dynamic_slice_in_dim(
            jnp.concatenate([flipped, flipped], axis=0), count - place, count, 0
        )

    def rolled(self, stacked, place):
        count = stacked.shape[0]
        return lax.dynamic_slice_in_dim(
            jnp.concatenate([stacked, stacked], axis=0), count - place, count, 0
        )

    def to_half(self, values):
        return self.move(
            values, lambda half, side, z, ring, core: (1 - half, side, z, ring, core)
        )

    def gather_teams(self, values):
        return lax.all_gather(values, ("half", "ring", "depth"), axis=0, tiled=True)

    def gather_rest(self, values):
        return lax.all_gather(values, ("ring", "depth"), axis=0, tiled=True)

    def scatter_half(self, values, *due):
        kept = lax.dynamic_index_in_dim(values, self.half, 0, keepdims=False)
        sent = lax.dynamic_index_in_dim(values, 1 - self.half, 0, keepdims=False)
        came = after(self.to_half(sent), *due)
        return (kept.astype(WIDE) + came.astype(WIDE)).astype(LOW)

    def scatter_teams(self, values):
        return lax.psum_scatter(
            values, ("half", "ring", "depth"), scatter_dimension=0, tiled=True
        )

    def scatter_rest(self, values):
        return lax.psum_scatter(values, ("ring", "depth"), scatter_dimension=0, tiled=True)

    def whole_columns(self, parts):
        parts = lax.all_to_all(parts, SQUARE, 0, 0, tiled=True)
        return parts.transpose(1, 0, 2).reshape(parts.shape[1], -1)

    def whole_rows(self, *packs):
        blocks = lax.axis_size(SQUARE)
        values = jnp.concatenate([pack for pack, _ in packs], axis=0)
        rows, columns = values.shape
        parts = values.reshape(rows, blocks, columns // blocks).transpose(1, 0, 2)
        parts = lax.all_to_all(parts, SQUARE, 0, 0, tiled=True)
        found, low = [], 0
        for pack, kinds in packs:
            share = pack.shape[0] // kinds
            part = parts[:, low : low + kinds * share].reshape(blocks, kinds, share, -1)
            found.append(part.transpose(1, 0, 2, 3).reshape(kinds, blocks * share, -1))
            low += kinds * share
        return found

    def gather_rows(self, values, *due):
        mate = self.to_rank(values, 1)
        across = after(self.to_rank(values, 2), *due)
        return [values, mate, across, self.to_rank(across, 1)]

    def scatter_rows(self, blocks, waiting=(), due=()):
        rows = blocks[0].shape[0]
        came = self.to_rank(jnp.concatenate([blocks[1], blocks[3]], axis=0).astype(LOW), 1)
        came, *waiting = lax.optimization_barrier((came, *waiting))
        across = (blocks[2].astype(WIDE) + came[rows:].astype(WIDE)).astype(LOW)
        own = blocks[0].astype(WIDE) + came[:rows].astype(WIDE)
        across = after(self.to_rank(across, 2), *due)
        return own + across.astype(WIDE), waiting

    def gather_square(self, values, *due):
        beside, opposite = self.to_rank(values, 2), self.to_half(values)
        rows = values.shape[0] // 2
        diagonal = jnp.concatenate(
            [self.to_half(beside[:rows]), self.to_rank(opposite[rows:], 2)], axis=0
        )
        diagonal = after(diagonal, *due)
        blocks = [values, beside, opposite, diagonal]
        return blocks + [self.to_rank(block, 1) for block in blocks]

    def scatter_square(self, values, waiting=(), due=()):
        size = values.shape[0] // 8
        rows = size // 2
        came = self.to_rank(values[4 * size :], 1)
        came, *waiting = lax.optimization_barrier((came, *waiting))
        sums = values[: 4 * size].astype(WIDE) + came.astype(WIDE)
        own, beside, opposite, diagonal = [sums[k * size : (k + 1) * size] for k in range(4)]
        diagonal = diagonal.astype(LOW)
        first = self.to_half(diagonal[:rows]).astype(WIDE)
        second = self.to_rank(diagonal[rows:], 2).astype(WIDE)
        beside = jnp.concatenate([beside[:rows] + first, beside[rows:]], axis=0).astype(LOW)
        opposite = jnp.concatenate([opposite[:rows], opposite[rows:] + second], axis=0).astype(LOW)
        beside, opposite = self.to_rank(beside, 2), self.to_half(opposite)
        beside = after(beside, *due)
        return own + beside.astype(WIDE) + opposite.astype(WIDE), waiting

    def total(self, values):
        sizes = (self.halves, 2, self.depth, self.rings, 2)
        for axis, size in enumerate(sizes):
            bit = 1
            while bit < size:
                values = values + self.move(
                    values, lambda *place: (*place[:axis], place[axis] ^ bit, *place[axis + 1 :])
                )
                bit *= 2
        return values


def after(values, *others):
    return lax.optimization_barrier((values, *others))[0]


def times(a, b):
    return lax.dot_general(a, b, (((1,), (0,)), ((), ())), preferred_element_type=WIDE)


def times_rows(a, b):
    return lax.dot_general(a, b, (((1,), (1,)), ((), ())), preferred_element_type=WIDE)


def columns_times(a, b):
    return lax.dot_general(a, b, (((0,), (0,)), ((), ())), preferred_element_type=WIDE)


def root_norm(values, gain_row):
    return (
        values * lax.rsqrt(jnp.mean(values * values, axis=-1, keepdims=True) + EPSILON) * gain_row
    )


def root_norm_back(inputs, gain_row, grad, arriving):
    widened = inputs.astype(WIDE)
    inverse = lax.rsqrt(jnp.mean(widened * widened, axis=-1, keepdims=True) + EPSILON)
    unit_rows = widened * inverse
    scaled = grad * gain_row
    through = inverse * (scaled - unit_rows * jnp.mean(scaled * unit_rows, axis=-1, keepdims=True))
    gain_grad = jnp.sum(grad * unit_rows, axis=0)
    return ((arriving.astype(WIDE) + through).astype(LOW), gain_grad)


def angles(offsets, head_width):
    inverse = ROTARY_BASE ** (-jnp.arange(0, head_width, 2).astype(WIDE) / head_width)
    phases = offsets.astype(WIDE)[:, None] * inverse[None, :]
    return (jnp.tile(jnp.cos(phases), (1, 4)), jnp.tile(jnp.sin(phases), (1, 4)))


def lanes(shape):
    return lax.broadcasted_iota(jnp.int32, shape, len(shape) - 1)


def pair_mean(values):
    width = values.shape[-1] // 2
    first = lanes(values.shape) < width
    low = jnp.sum(jnp.where(first, values, 0), axis=-1, keepdims=True)
    high = jnp.sum(jnp.where(first, 0, values), axis=-1, keepdims=True)
    return jnp.where(first, low, high) / width


def turned(values):
    width = values.shape[-1]
    quarter = width // 4
    ahead = pltpu.roll(values, width - quarter, 1)
    behind = pltpu.roll(values, quarter, 1)
    return jnp.where(lanes(values.shape) % (width // 2) < quarter, -ahead, behind)


def unit_pair(values):
    inverse = lax.rsqrt(pair_mean(values * values) + EPSILON)
    return values * inverse, inverse


def rotated(values, gain_row, cosine, sine):
    unit, _ = unit_pair(values)
    scaled = unit * gain_row
    return scaled * cosine + turned(scaled) * sine


def rotated_back(values, gain_row, cosine, sine, grad):
    unit, inverse = unit_pair(values)
    scaled_grad = grad * cosine - turned(grad * sine)
    unit_grad = scaled_grad * gain_row
    result = inverse * (unit_grad - unit * pair_mean(unit_grad * unit))
    return result, jnp.sum(scaled_grad * unit, axis=0, keepdims=True)


def heads_kernel(packed_ref, gains_ref, cosine_ref, sine_ref, queries_ref, pairs_ref):
    width = cosine_ref.shape[1]
    cosine, sine = cosine_ref[...], sine_ref[...]
    for g in range(packed_ref.shape[1] // (2 * width)):
        own = slice(g * width, (g + 1) * width)
        values = packed_ref[:, 2 * g * width : (2 * g + 1) * width]
        queries_ref[:, own] = rotated(values, gains_ref[0:1], cosine, sine).astype(LOW)
        values = packed_ref[:, (2 * g + 1) * width : (2 * g + 2) * width]
        keys = rotated(values, gains_ref[1:2], cosine, sine)
        first = lanes(values.shape) < width // 2
        pairs_ref[:, own] = jnp.where(first, keys, values).astype(LOW)


def heads_back_kernel(
    packed_ref, gains_ref, cosine_ref, sine_ref, queries_grad_ref, pairs_grad_ref, out_ref, gain_ref
):
    width = cosine_ref.shape[1]
    cosine, sine = cosine_ref[...], sine_ref[...]

    @pl.when(pl.program_id(0) == 0)
    def _():
        gain_ref[...] = jnp.zeros_like(gain_ref)

    for g in range(packed_ref.shape[1] // (2 * width)):
        own = slice(g * width, (g + 1) * width)
        for part, grad_ref in ((0, queries_grad_ref), (1, pairs_grad_ref)):
            place = slice((2 * g + part) * width, (2 * g + part + 1) * width)
            grad = grad_ref[:, own].astype(WIDE)
            result, gain_grad = rotated_back(
                packed_ref[:, place], gains_ref[part : part + 1], cosine, sine, grad
            )
            if part:
                result = jnp.where(lanes(result.shape) < width // 2, result, grad)
            out_ref[:, place] = result.astype(LOW)
            gain_ref[part : part + 1] += gain_grad


def split_heads(packed, gains, cosine, sine, rows):
    total, columns = packed.shape
    width = cosine.shape[1]
    row_block = lambda size: pl.BlockSpec((rows, size), lambda i: (i, 0))
    return pl.pallas_call(
        heads_kernel,
        grid=(total // rows,),
        in_specs=[
            row_block(columns),
            pl.BlockSpec((2, width), lambda i: (0, 0)),
            row_block(width),
            row_block(width),
        ],
        out_specs=[row_block(columns // 2), row_block(columns // 2)],
        out_shape=[jax.ShapeDtypeStruct((total, columns // 2), LOW)] * 2,
        compiler_params=pltpu.CompilerParams(vmem_limit_bytes=48 << 20),
        name="heads",
    )(packed, gains, cosine, sine)


def split_heads_back(packed, gains, cosine, sine, queries_grad, pairs_grad, rows):
    total, columns = packed.shape
    width = cosine.shape[1]
    row_block = lambda size: pl.BlockSpec((rows, size), lambda i: (i, 0))
    return pl.pallas_call(
        heads_back_kernel,
        grid=(total // rows,),
        in_specs=[
            row_block(columns),
            pl.BlockSpec((2, width), lambda i: (0, 0)),
            row_block(width),
            row_block(width),
            row_block(columns // 2),
            row_block(columns // 2),
        ],
        out_specs=[row_block(columns), pl.BlockSpec((2, width), lambda i: (0, 0))],
        out_shape=[
            jax.ShapeDtypeStruct((total, columns), LOW),
            jax.ShapeDtypeStruct((2, width), WIDE),
        ],
        compiler_params=pltpu.CompilerParams(vmem_limit_bytes=48 << 20),
        name="heads_back",
    )(packed, gains, cosine, sine, queries_grad, pairs_grad)


def block_weights(offsets, queries, keys, scale):
    scores = (
        lax.dot_general(queries, keys, (((1,), (1,)), ((), ())), preferred_element_type=WIDE)
        * scale
    )
    rows, window = offsets.shape[0], keys.shape[0]
    shape = (rows, window)
    back = (
        lax.broadcasted_iota(jnp.int32, shape, 0)
        + LONGEST
        - lax.broadcasted_iota(jnp.int32, shape, 1)
    )
    allowed = (back >= 0) & (back <= offsets)
    allowed = jnp.concatenate([allowed.astype(WIDE)] * (queries.shape[0] // rows), axis=0) > 0.5
    scores = jnp.where(allowed, scores, NEGATIVE)
    weights = jnp.exp(scores - jnp.max(scores, axis=-1, keepdims=True))
    return weights / jnp.sum(weights, axis=-1, keepdims=True)


def over(values):
    width = values.shape[1] // 2
    return jnp.concatenate([values[:, :width], values[:, width:]], axis=0)


def beside(values):
    rows = values.shape[0] // 2
    return jnp.concatenate([values[:rows], values[rows:]], axis=1)


def attend_kernel(scale, offsets_ref, queries_ref, pairs_ref, out_ref):
    rows, width = queries_ref.shape[0], queries_ref.shape[1] // 2
    low = pl.multiple_of(pl.program_id(1) * rows, rows)
    pairs = pairs_ref[pl.ds(low, LONGEST + rows), :]
    weights = block_weights(offsets_ref[...], over(queries_ref[...]), pairs[:, :width], scale)
    result = jnp.dot(weights.astype(LOW), pairs[:, width:], preferred_element_type=WIDE)
    out_ref[...] = beside(result.astype(LOW))


def attend_back_kernel(
    scale, offsets_ref, queries_ref, pairs_ref, grad_ref, queries_grad_ref, pairs_grad_ref
):
    rows, width = queries_ref.shape[0], queries_ref.shape[1] // 2

    @pl.when(pl.program_id(1) == 0)
    def _():
        pairs_grad_ref[...] = jnp.zeros_like(pairs_grad_ref)

    low = pl.multiple_of(pl.program_id(1) * rows, rows)
    window = pl.ds(low, LONGEST + rows)
    queries, grad = over(queries_ref[...]), over(grad_ref[...])
    pairs = pairs_ref[window, :]
    keys, values = pairs[:, :width], pairs[:, width:]
    weights = block_weights(offsets_ref[...], queries, keys, scale)
    flow = lax.dot_general(grad, values, (((1,), (1,)), ((), ())), preferred_element_type=WIDE)
    inner = jnp.sum(weights * flow, axis=-1, keepdims=True)
    score_grad = (weights * (flow - inner)).astype(LOW)
    values_grad = lax.dot_general(
        weights.astype(LOW), grad, (((0,), (0,)), ((), ())), preferred_element_type=WIDE
    )
    keys_grad = lax.dot_general(
        score_grad, queries, (((0,), (0,)), ((), ())), preferred_element_type=WIDE
    )
    pairs_grad_ref[window, :] += jnp.concatenate([keys_grad * scale, values_grad], axis=1)
    queries_grad = jnp.dot(score_grad, keys, preferred_element_type=WIDE) * scale
    queries_grad_ref[...] = beside(queries_grad.astype(LOW))


def attention_specs(queries, pairs, rows, head_width):
    width = 2 * head_width
    grid = (queries.shape[1] // width, queries.shape[0] // rows)
    offsets_spec = pl.BlockSpec((rows, 1), lambda g, i: (i, 0))
    rows_spec = pl.BlockSpec((rows, width), lambda g, i: (i, g))
    pairs_spec = pl.BlockSpec((pairs.shape[0], width), lambda g, i: (0, g))
    return (grid, offsets_spec, rows_spec, pairs_spec)


def attend(offsets, queries, pairs, rows, head_width):
    grid, offsets_spec, rows_spec, pairs_spec = attention_specs(queries, pairs, rows, head_width)
    return pl.pallas_call(
        functools.partial(attend_kernel, head_width ** (-0.5)),
        grid=grid,
        in_specs=[offsets_spec, rows_spec, pairs_spec],
        out_specs=rows_spec,
        out_shape=jax.ShapeDtypeStruct(queries.shape, LOW),
        compiler_params=pltpu.CompilerParams(vmem_limit_bytes=48 << 20),
        name="attend",
    )(offsets[:, None], queries, pairs)


def attend_back(offsets, queries, pairs, grad, rows, head_width):
    grid, offsets_spec, rows_spec, pairs_spec = attention_specs(queries, pairs, rows, head_width)
    return pl.pallas_call(
        functools.partial(attend_back_kernel, head_width ** (-0.5)),
        grid=grid,
        in_specs=[offsets_spec, rows_spec, pairs_spec, rows_spec],
        out_specs=[rows_spec, pairs_spec],
        out_shape=[
            jax.ShapeDtypeStruct(queries.shape, LOW),
            jax.ShapeDtypeStruct(pairs.shape, WIDE),
        ],
        compiler_params=pltpu.CompilerParams(vmem_limit_bytes=48 << 20),
        name="attend_back",
    )(offsets[:, None], queries, pairs, grad)


def whole_rows_of(ref):
    teams, rows, columns = ref.shape
    return ref[...].reshape(teams * rows, columns)


def dot_nt(a, b):
    return lax.dot_general(a, b, (((1,), (1,)), ((), ())), preferred_element_type=WIDE)


def feed_kernel(
    normed_ref, gate_ref, up_ref, outward_ref, gated_ref, raised_ref, hidden_ref, update_ref
):
    normed = normed_ref[...]
    gate = dot_nt(normed, whole_rows_of(gate_ref))
    up = dot_nt(normed, whole_rows_of(up_ref))
    gated_ref[...] = gate.astype(LOW)
    raised_ref[...] = up.astype(LOW)
    hidden = (gate / (1 + jnp.exp(-gate)) * up).astype(LOW)
    hidden_ref[...] = hidden
    update_ref[...] = jnp.dot(
        hidden, whole_rows_of(outward_ref), preferred_element_type=WIDE
    ).astype(LOW)


def feed_back_kernel(
    full_ref,
    gated_ref,
    raised_ref,
    gate_ref,
    up_ref,
    outward_ref,
    gate_grad_ref,
    up_grad_ref,
    update_ref,
):
    hidden_grad = dot_nt(full_ref[...], whole_rows_of(outward_ref))
    gate = gated_ref[...].astype(WIDE)
    up = raised_ref[...].astype(WIDE)
    sigmoid = 1 / (1 + jnp.exp(-gate))
    through = hidden_grad * sigmoid
    gate_grad = (through * up * (1 + gate * (1 - sigmoid))).astype(LOW)
    up_grad = (through * gate).astype(LOW)
    gate_grad_ref[...] = gate_grad
    up_grad_ref[...] = up_grad
    update = jnp.dot(gate_grad, whole_rows_of(gate_ref), preferred_element_type=WIDE)
    update += jnp.dot(up_grad, whole_rows_of(up_ref), preferred_element_type=WIDE)
    update_ref[...] = update.astype(LOW)


def feed_grads_kernel(
    gate_grad_ref, up_grad_ref, hidden_ref, normed_ref, full_ref, out_ref, total_ref
):
    teams, rows, columns = out_ref.shape
    width, step = teams * rows, 128

    def fill(left_ref, right_ref):
        for low in range(0, width, step):
            own = slice(low, min(low + step, width))
            total_ref[own] = lax.dot_general(
                left_ref[:, own],
                right_ref[...],
                (((0,), (0,)), ((), ())),
                preferred_element_type=WIDE,
            )
        out_ref[...] = total_ref[...].astype(LOW).reshape(teams, rows, columns)

    pl.when(pl.program_id(0) == 0)(lambda: fill(gate_grad_ref, normed_ref))
    pl.when(pl.program_id(0) == 1)(lambda: fill(up_grad_ref, normed_ref))
    pl.when(pl.program_id(0) == 2)(lambda: fill(hidden_ref, full_ref))


def kind_spec(pack, k):
    teams, _, rows, columns = pack.shape
    return pl.BlockSpec((teams, None, rows, columns), lambda i: (0, k, 0, 0))


def row_spec(rows, columns):
    return pl.BlockSpec((rows, columns), lambda i: (i, 0))


def feed_call(normed, pack, rows):
    total, columns = normed.shape
    width = pack.shape[0] * pack.shape[2]
    wide = jax.ShapeDtypeStruct((total, width), LOW)
    return pl.pallas_call(
        feed_kernel,
        grid=(total // rows,),
        in_specs=[row_spec(rows, columns)] + [kind_spec(pack, k) for k in range(3)],
        out_specs=[row_spec(rows, width)] * 3 + [row_spec(rows, columns)],
        out_shape=[wide] * 3 + [jax.ShapeDtypeStruct((total, columns), LOW)],
        compiler_params=pltpu.CompilerParams(vmem_limit_bytes=48 << 20),
        name="feed",
    )(normed, pack, pack, pack)


def feed_back_call(full, gated, raised, pack, rows):
    total, columns = full.shape
    width = gated.shape[1]
    wide = jax.ShapeDtypeStruct((total, width), LOW)
    return pl.pallas_call(
        feed_back_kernel,
        grid=(total // rows,),
        in_specs=[row_spec(rows, columns)]
        + [row_spec(rows, width)] * 2
        + [kind_spec(pack, k) for k in range(3)],
        out_specs=[row_spec(rows, width)] * 2 + [row_spec(rows, columns)],
        out_shape=[wide] * 2 + [jax.ShapeDtypeStruct((total, columns), LOW)],
        compiler_params=pltpu.CompilerParams(vmem_limit_bytes=48 << 20),
        name="feed_back",
    )(full, gated, raised, pack, pack, pack)


def feed_grads_call(gate_grad, up_grad, hidden, normed, full, teams):
    total, columns = normed.shape
    width = hidden.shape[1]
    wide_spec = pl.BlockSpec((total, width), lambda k: (0, 0))
    rows_spec = pl.BlockSpec((total, columns), lambda k: (0, 0))
    return pl.pallas_call(
        feed_grads_kernel,
        grid=(3,),
        in_specs=[wide_spec] * 3 + [rows_spec] * 2,
        out_specs=pl.BlockSpec((teams, None, width // teams, columns), lambda k: (0, k, 0, 0)),
        out_shape=jax.ShapeDtypeStruct((teams, 3, width // teams, columns), LOW),
        scratch_shapes=[pltpu.VMEM((width, columns), WIDE)],
        compiler_params=pltpu.CompilerParams(vmem_limit_bytes=58 << 20),
        name="feed_grads",
    )(gate_grad, up_grad, hidden, normed, full)


def local(
    tokens,
    lengths,
    gains,
    qk_gains,
    conv_kernel,
    conv_in,
    conv_out,
    ffn1_in,
    ffn1_out,
    attn_qkv,
    attn_out,
    ffn2_in,
    ffn2_out,
    cotangent,
):
    here = Place()
    depth = here.depth
    stretch = tokens.shape[1]
    slice_width = tokens.shape[2]
    model_width = slice_width * depth
    sections = 2 * here.halves
    stream_rows = sections * stretch
    team_rows = stream_rows // depth
    own_rows = team_rows // RANKS
    head_width = attn_qkv.shape[2] // 4
    groups_here = attn_qkv.shape[1]
    groups = groups_here * depth // RANKS
    block_width = conv_in.shape[0]
    query_rows = min(256, team_rows)
    spare = depth // RANKS

    def row_goal(k):
        def goal(half, side, z, ring, core):
            part = (z + k) % depth
            rank = part % RANKS
            batch = half * 2 + side
            return (core, rank // 2, batch * spare + part // RANKS, ring, rank % 2)

        return goal

    own_part = (here.z % spare) * RANKS + here.rank

    def row_pieces(values):
        grid = values.reshape(depth, own_rows, slice_width)
        return [
            here.move(
                lax.dynamic_index_in_dim(grid, (here.z + k) % depth, 0, keepdims=False),
                row_goal(k),
            )
            for k in range(depth)
        ]

    def rows_in(pieces):
        columns = here.mirrored(jnp.stack(lax.optimization_barrier(tuple(pieces))), own_part)
        return columns.transpose(1, 0, 2).reshape(own_rows, model_width)

    def rows_out(*arrays):
        count = len(arrays)
        grid = jnp.concatenate(arrays, axis=0).reshape(count * own_rows, depth, slice_width)
        grid = grid.transpose(1, 0, 2)
        pieces = []
        for k in range(depth):
            piece = lax.dynamic_index_in_dim(grid, (own_part - k) % depth, 0, keepdims=False)
            route = [(goal, source) for source, goal in here.route(row_goal(k))]
            pieces.append(lax.ppermute(piece, AXES, route))
        rows = here.rolled(jnp.stack(pieces), here.z)
        rows = rows.reshape(depth, count, own_rows, slice_width).transpose(1, 0, 2, 3)
        return list(rows.reshape(count, 1, stretch, slice_width))

    def inward(values):
        return values.transpose(1, 2, 0)

    def by_square(values):
        kinds, rows, columns = values.shape
        blocks = lax.axis_size(SQUARE)
        parts = values.reshape(kinds, blocks, rows // blocks, columns).transpose(1, 0, 2, 3)
        return parts.reshape(blocks, kinds * (rows // blocks), columns)

    rest = here.rings * depth
    teams = here.halves * rest

    def split_kinds(values, kinds):
        grid = values.reshape(here.halves, rest, kinds, -1, model_width)
        return [grid[:, :, k].reshape(-1, model_width) for k in range(kinds)]

    def halves_sum(grads, *due):
        grids = [grad.astype(LOW).reshape(here.halves, rest, -1, model_width) for grad in grads]
        return here.scatter_half(
            jnp.concatenate(grids, axis=2).reshape(here.halves, -1, model_width), *due
        )

    taps = conv_kernel.shape[0]
    square = lax.axis_index(SQUARE)
    share = slice_width // lax.axis_size(SQUARE)
    channels = teams * share

    heads_rows = attn_out.shape[0] // groups_here
    heads_size = attn_qkv.shape[2] + heads_rows

    def heads_goal(half, side, z, ring, core):
        rank = z // spare
        return (half, rank // 2, (2 * side + core) * spare + z % spare, ring, rank % 2)

    heads_part = jnp.concatenate(
        [inward(attn_qkv), attn_out.reshape(groups_here, heads_rows, -1)], axis=1
    )
    heads_flat = heads_part.shape[0] * heads_part.shape[1]
    heads_moved = here.move(heads_part.reshape(heads_flat, block_width), heads_goal)

    def heads_unpack(gathered):
        blocks = gathered.reshape(
            here.halves, here.rings, 2, 2, spare, groups_here * heads_size, block_width
        )
        ordered = [
            blocks[half, ring, side, core].reshape(groups * heads_size, block_width)
            for half in range(here.halves)
            for side in range(2)
            for ring in range(here.rings)
            for core in range(2)
        ]
        weights = jnp.concatenate(ordered, axis=1).reshape(groups, heads_size, model_width)
        return (
            weights[:, : heads_size - heads_rows].reshape(-1, model_width),
            weights[:, heads_size - heads_rows :].reshape(-1, model_width),
        )

    def heads_rows_of(inward_grad, outward_grad):
        grad = jnp.concatenate(
            [
                inward_grad.astype(LOW).reshape(groups, -1, model_width),
                outward_grad.astype(LOW).reshape(groups, -1, model_width),
            ],
            axis=1,
        ).reshape(groups * heads_size, model_width)
        blocks = [
            grad[:, block_width * k : block_width * (k + 1)]
            for k in range(model_width // block_width)
        ]
        ordered = [
            blocks[((half * 2 + side) * here.rings + ring) * 2 + core]
            for half in range(here.halves)
            for ring in range(here.rings)
            for side in range(2)
            for core in range(2)
        ]
        return jnp.concatenate(ordered, axis=0)

    mixer_flat = 4 * share
    feed_rows = 3 * ffn1_out.shape[0] // lax.axis_size(SQUARE)
    mixer_whole = here.whole_columns(
        by_square(jnp.concatenate([inward(conv_in), conv_out[None]], axis=0))
    )
    residual = rows_in(row_pieces(after(tokens, mixer_whole)))
    own_taps = lax.dynamic_slice_in_dim(conv_kernel, square * share, share, 1)
    own_taps = jnp.pad(own_taps, ((0, 16 - taps), (0, model_width - share)))
    mixer_teams = here.gather_teams(jnp.concatenate([mixer_whole, own_taps], axis=0))
    feed_packs = [
        by_square(jnp.concatenate([inward(inner), outer[None]], axis=0))
        for inner, outer in ((ffn1_in, ffn1_out), (ffn2_in, ffn2_out))
    ]
    feed_parts = here.whole_columns(after(jnp.concatenate(feed_packs, axis=1), mixer_whole))
    mixer_part = mixer_teams.reshape(here.halves, rest, -1, model_width)
    mixer_weights = jnp.concatenate(
        split_kinds(mixer_part[:, :, :mixer_flat].reshape(-1, model_width), 4), axis=0
    )
    mixer_inward, mixer_outward = mixer_weights[: 3 * channels], mixer_weights[3 * channels :]
    kernel = (
        mixer_part[:, :, mixer_flat : mixer_flat + taps, :share]
        .transpose(2, 0, 1, 3)
        .reshape(taps, channels)
        .astype(WIDE)
    )

    aligned = feed_rows % 48 == 0
    out_rows = feed_rows // 3

    def feed_pack(gathered):
        pack = gathered.reshape(-1, 3, out_rows, model_width)
        if aligned:
            return pack
        return pack.transpose(1, 0, 2, 3).reshape(1, 3, -1, model_width)

    def feed_teams_of(grad):
        if not aligned:
            grad = grad.reshape(3, -1, out_rows, model_width).transpose(1, 0, 2, 3)
        return grad.reshape(-1, model_width)

    first_rest = here.gather_rest(after(feed_parts[:feed_rows], mixer_teams, residual))
    first_pack = feed_pack(first_rest)

    own_lengths = jnp.where(here.half == here.core, lengths[0], here.to_rank(lengths[0], 1))
    places = here.z * team_rows + jnp.arange(team_rows + 2, dtype=jnp.int32)
    passed = (places[:, None] >= jnp.cumsum(own_lengths)[None, :]).astype(jnp.int32)
    offsets = places - jnp.sum(passed * own_lengths[None, :], axis=1)
    first_mask = (offsets >= 1).astype(WIDE)[:, None]
    second_mask = (offsets >= 2).astype(WIDE)[:, None]
    offsets = offsets[:team_rows]
    cosine_rows, sine_rows = angles(offsets, head_width)
    beside_gains = here.to_rank(gains, 2)
    half_gains = jnp.where(
        here.side == 0,
        jnp.concatenate([gains, beside_gains]),
        jnp.concatenate([beside_gains, gains]),
    )
    all_gains = half_gains
    if here.halves > 1:
        other_gains = here.to_half(half_gains)
        all_gains = jnp.where(
            here.half == 0,
            jnp.concatenate([half_gains, other_gains]),
            jnp.concatenate([other_gains, half_gains]),
        )
    pair_gains = jnp.tile(qk_gains, (1, 2))

    def gather_ordered(values, *due):
        return jnp.concatenate(here.by_rank(here.gather_rows(values, *due)), axis=0)

    def gather_any(values, *due):
        return jnp.concatenate(here.gather_rows(values, *due), axis=0)

    def scatter_ordered(values, waiting=(), due=()):
        grid = values.astype(LOW).reshape(RANKS, own_rows, model_width)
        blocks = [
            lax.dynamic_index_in_dim(grid, jnp.bitwise_xor(here.rank, k), 0, keepdims=False)
            for k in range(RANKS)
        ]
        return here.scatter_rows(blocks, waiting, due)

    def scatter_any(values, waiting=(), due=()):
        grid = values.astype(LOW).reshape(RANKS, own_rows, model_width)
        return here.scatter_rows([grid[k] for k in range(RANKS)], waiting, due)

    def joined(residual, update):
        return (residual.astype(WIDE) + update).astype(LOW)

    def mixer_forward(residual):
        normed = gather_ordered(root_norm(residual.astype(WIDE), all_gains[0]).astype(LOW))
        projected = times_rows(normed, mixer_inward)
        before, gate, behind = (
            projected[:, :channels],
            projected[:, channels : 2 * channels],
            projected[:, 2 * channels :],
        )
        product = before * behind
        tail = here.up(product[-2:], 1)
        extended = jnp.concatenate([tail, product], axis=0)
        once = extended[1:-1] * first_mask[:team_rows]
        twice = extended[:-2] * second_mask[:team_rows]
        mixed = kernel[2] * product + kernel[1] * once + kernel[0] * twice
        gated = (gate * mixed).astype(LOW)
        update, _ = scatter_ordered(times(gated, mixer_outward))
        return joined(residual, update), (
            residual, normed, before, gate, behind, product, once, twice, mixed, gated,
        )

    def mixer_backward(arriving, saved, *due):
        residual, normed, before, gate, behind, product, once, twice, mixed, gated = saved
        full = gather_ordered(arriving, *due)
        gated_grad = times_rows(full, mixer_outward)
        gate_grad = gated_grad * mixed
        mixed_grad = gated_grad * gate
        following = here.up(mixed_grad[:2], -1)
        extended = jnp.concatenate([mixed_grad, following], axis=0)
        product_grad = (
            kernel[2] * mixed_grad
            + kernel[1] * extended[1:-1] * first_mask[1:-1]
            + kernel[0] * extended[2:] * second_mask[2:]
        )
        kernel_grad = jnp.stack(
            [
                jnp.sum(mixed_grad * twice, axis=0),
                jnp.sum(mixed_grad * once, axis=0),
                jnp.sum(mixed_grad * product, axis=0),
            ]
        )
        low = jnp.concatenate(
            [product_grad * behind, gate_grad, product_grad * before], axis=1
        ).astype(LOW)
        update, (low, full) = scatter_ordered(times(low, mixer_inward), (low, full))
        grad = [columns_times(low[:, k * channels : (k + 1) * channels], normed) for k in range(3)]
        grad.append(columns_times(gated, full))
        leaving, gain_grad = root_norm_back(residual, all_gains[0], update, arriving)
        return leaving, gain_grad, kernel_grad, grad, low

    def square_rows(values, *due):
        return jnp.concatenate(here.gather_square(values, *due), axis=0)

    def square_sums(values, waiting=(), due=()):
        return here.scatter_square(values.astype(LOW), waiting, due)

    def feed_forward(residual, gain_row, pack, gather, *due):
        normed = gather(root_norm(residual.astype(WIDE), gain_row).astype(LOW), *due)
        gated, raised, hidden, update = feed_call(normed, pack, query_rows)
        return update, (residual, normed, gated, raised, hidden)

    def feed_joined(residual, update, scatter, due=()):
        return joined(residual, scatter(update, (), due)[0])

    def feed_backward(arriving, saved, gain_row, pack, gather, scatter, *due):
        residual, normed, gated, raised, hidden = saved
        full = gather(arriving, *due)
        gate_grad, up_grad, update = feed_back_call(full, gated, raised, pack, query_rows)
        update, (gate_grad, up_grad, full) = scatter(update, (gate_grad, up_grad, full))
        grad = feed_grads_call(gate_grad, up_grad, hidden, normed, full, pack.shape[0])
        update = after(update, grad)
        leaving, gain_grad = root_norm_back(residual, gain_row, update, arriving)
        return leaving, gain_grad, feed_teams_of(grad)

    halo_steps = LONGEST // team_rows

    def heads_forward(residual, due):
        normed = root_norm(residual.astype(WIDE), all_gains[2]).astype(LOW)
        normed = gather_ordered(normed, *due[0])
        packed = times_rows(normed, heads_inward)
        queries, pairs = split_heads(packed, pair_gains, cosine_rows, sine_rows, query_rows)
        window = jnp.concatenate(
            [here.up(pairs, step) for step in range(halo_steps, 0, -1)] + [pairs], axis=0
        )
        window = after(window, *due[1])
        attended = attend(offsets, queries, window, query_rows, head_width)
        update, _ = scatter_ordered(times(attended, heads_outward), (), due[2])
        return joined(residual, update), (residual, normed, packed, queries, window, attended)

    def heads_backward(arriving, saved):
        residual, normed, packed, queries, window, attended = saved
        full = gather_ordered(arriving)
        attended_grad = times_rows(full, heads_outward).astype(LOW)
        queries_grad, pairs_grad = attend_back(
            offsets, queries, window, attended_grad, query_rows, head_width
        )
        own = pairs_grad[LONGEST:]
        for step in range(1, halo_steps + 1):
            low = (halo_steps - step) * team_rows
            moved = here.up(pairs_grad[low : low + team_rows].astype(LOW), -step)
            own = own + moved.astype(WIDE)
        own = own.astype(LOW)
        low, pair_gains_grad = split_heads_back(
            packed, pair_gains, cosine_rows, sine_rows, queries_grad, own, query_rows
        )
        update, (low, full) = scatter_ordered(times(low, heads_inward), (low, full))
        inward_grad = columns_times(low, normed)
        outward_grad = columns_times(attended, full)
        leaving, gain_grad = root_norm_back(residual, all_gains[2], update, arriving)
        width = head_width
        head_gains_grad = jnp.stack(
            [pair_gains_grad[0, :width] + pair_gains_grad[0, width:], pair_gains_grad[1, :width]]
        )
        return leaving, gain_grad, head_gains_grad, inward_grad, outward_grad, own

    residual, mixer_saved = mixer_forward(residual)
    heads_teams = here.gather_teams(after(heads_moved, first_rest, residual))
    heads_inward, heads_outward = heads_unpack(heads_teams)
    update, first_saved = feed_forward(residual, all_gains[1], first_pack, square_rows)
    residual = feed_joined(residual, update, square_sums)
    second_teams = here.gather_teams(after(feed_parts[feed_rows:], heads_teams, update))
    second_pack = feed_pack(second_teams)
    pieces = row_pieces(after(cotangent, residual))
    residual, heads_saved = heads_forward(
        residual, [(heads_inward, heads_outward, *pieces[:1]), pieces[1:2], pieces[2:3]]
    )
    last_update, second_saved = feed_forward(
        residual, all_gains[3], second_pack, gather_any, *pieces[3:]
    )
    flowing = rows_in(pieces)

    flowing, gain3, second_grad = feed_backward(
        flowing, second_saved, all_gains[3], second_pack, gather_any, scatter_any
    )
    second_sum = here.scatter_teams(after(second_grad, flowing))
    flowing, gain2, head_gains_grad, heads_inward_grad, heads_outward_grad, _ = heads_backward(
        flowing, heads_saved
    )
    output = feed_joined(residual, after(last_update, flowing), scatter_any)
    heads_grad = heads_rows_of(heads_inward_grad, heads_outward_grad)
    heads_half = here.scatter_half(heads_grad.reshape(here.halves, -1, block_width))
    flowing, gain1, first_grad = feed_backward(
        flowing,
        first_saved,
        all_gains[1],
        first_pack,
        square_rows,
        square_sums,
        heads_grad,
    )
    first_sum = here.scatter_rest(after(first_grad, flowing, second_sum))
    flowing, gain0, kernel_grad, mixer_grad, low = mixer_backward(
        flowing, mixer_saved, output
    )
    mixer_half = halves_sum([mixer_grad[k] for k in range(4)])
    output, input_grad = rows_out(output, after(flowing, mixer_half))
    late = [part.reshape(rest, -1, model_width) for part in (heads_half, mixer_half)]
    late_sum = here.scatter_rest(
        after(jnp.concatenate(late, axis=1).reshape(-1, model_width), first_sum)
    )
    (second_grad,) = here.whole_rows((after(second_sum, input_grad), 3))

    heads_route = [(b, a) for a, b in here.route(heads_goal)]
    (first_grad,) = here.whole_rows((after(first_sum, second_grad), 3))
    heads_wide = heads_flat * block_width // model_width
    heads_grad = late_sum[:heads_wide].reshape(heads_flat, block_width)
    heads_grad = lax.ppermute(heads_grad, AXES, heads_route).reshape(heads_part.shape)
    (mixer_grad,) = here.whole_rows((late_sum[heads_wide:], 4))

    def outside(values):
        return values.transpose(2, 0, 1).astype(WIDE)

    kernel_blocks = kernel_grad.reshape(taps, here.halves, 1, here.rings, depth, 1, share)
    sides = (jnp.arange(2) == here.side).astype(WIDE).reshape(2, 1, 1, 1, 1)
    cores = (jnp.arange(2) == here.core).astype(WIDE).reshape(2, 1)
    kernel_whole = (kernel_blocks * sides * cores).transpose(0, 4, 1, 2, 3, 5, 6)
    small = jnp.concatenate(
        [
            jnp.stack([gain0, gain1, gain2, gain3]).reshape(-1),
            kernel_whole.reshape(-1),
            head_gains_grad.reshape(-1),
        ]
    )
    small = here.total(after(small, input_grad))
    gain_size, kernel_size = 4 * model_width, taps * model_width
    return (
        output,
        input_grad,
        small[:gain_size].reshape(4, model_width),
        small[gain_size + kernel_size :].reshape(2, head_width),
        small[gain_size : gain_size + kernel_size].reshape(taps, model_width),
        outside(mixer_grad[:3]),
        mixer_grad[3].astype(WIDE),
        outside(first_grad[:2]),
        first_grad[2].astype(WIDE),
        outside(heads_grad[:, : heads_size - heads_rows]),
        heads_grad[:, heads_size - heads_rows :].reshape(attn_out.shape).astype(WIDE),
        outside(second_grad[:2]),
        second_grad[2].astype(WIDE),
    )


def solution(mesh):
    sections, depth, replicas = mesh.devices.shape
    fine = Mesh(mesh.devices.reshape(sections // 2, 2, depth, replicas // 2, 2), AXES)
    rows = P(SQUARE, None, "depth")
    columns = P("depth", SQUARE)
    heads = P(SQUARE, "depth", None)
    stream = P(("half", "side"), ("ring", "core"), "depth")
    return jax.shard_map(
        local,
        mesh=fine,
        in_specs=(
            stream,
            P(("ring", "core"), None),
            P(("half", "side"), None),
            P(),
            P(None, "depth"),
            rows,
            columns,
            rows,
            columns,
            heads,
            columns,
            rows,
            columns,
            stream,
        ),
        out_specs=(
            stream,
            stream,
            P(),
            P(),
            P(),
            rows,
            columns,
            rows,
            columns,
            heads,
            columns,
            rows,
            columns,
        ),
        check_vma=False,
    )
```

```python
import functools

import jax
import jax.numpy as jnp
from jax import lax
from jax.experimental import pallas as pl
from jax.experimental.pallas import tpu as pltpu
from jax.sharding import Mesh
from jax.sharding import PartitionSpec as P

EPSILON = 1e-05
ROTARY_BASE = 1000000.0
NEGATIVE = -1e30
AXES = ("half", "side", "depth", "ring", "core")
SQUARE = ("half", "side", "ring", "core")
LOW = jnp.bfloat16
WIDE = jnp.float32
RANKS = 4
LONGEST = 1024


class Place:
    def __init__(self):
        self.halves = lax.axis_size("half")
        self.depth = lax.axis_size("depth")
        self.rings = lax.axis_size("ring")
        self.half = lax.axis_index("half")
        self.side = lax.axis_index("side")
        self.z = lax.axis_index("depth")
        self.ring = lax.axis_index("ring")
        self.core = lax.axis_index("core")
        self.rank = 2 * self.side + self.core

    def places(self):
        return [
            (half, side, z, ring, core)
            for half in range(self.halves)
            for side in range(2)
            for z in range(self.depth)
            for ring in range(self.rings)
            for core in range(2)
        ]

    def flat(self, half, side, z, ring, core):
        return (((half * 2 + side) * self.depth + z) * self.rings + ring) * 2 + core

    def route(self, target):
        pairs = [(place, target(*place)) for place in self.places()]
        return [(self.flat(*a), self.flat(*b)) for a, b in pairs if b is not None]

    def move(self, values, target):
        return lax.ppermute(values, AXES, self.route(target))

    def to_rank(self, values, k):
        return self.move(
            values, lambda half, side, z, ring, core: (half, side ^ (k >> 1), z, ring, core ^ (k & 1))
        )

    def up(self, values, distance=1):
        return self.move(
            values,
            lambda half, side, z, ring, core: (half, side, z + distance, ring, core)
            if 0 <= z + distance < self.depth
            else None,
        )

    def by_rank(self, blocks):
        return [
            lax.select_n(jnp.bitwise_xor(self.rank, b), *blocks) for b in range(RANKS)
        ]

    def mirrored(self, stacked, place):
        count = stacked.shape[0]
        flipped = jnp.concatenate([stacked[:1], stacked[:0:-1]], axis=0)
        return lax.dynamic_slice_in_dim(
            jnp.concatenate([flipped, flipped], axis=0), count - place, count, 0
        )

    def rolled(self, stacked, place):
        count = stacked.shape[0]
        return lax.dynamic_slice_in_dim(
            jnp.concatenate([stacked, stacked], axis=0), count - place, count, 0
        )

    def to_half(self, values):
        return self.move(
            values, lambda half, side, z, ring, core: (1 - half, side, z, ring, core)
        )

    def gather_teams(self, values):
        return lax.all_gather(values, ("half", "ring", "depth"), axis=0, tiled=True)

    def gather_rest(self, values):
        return lax.all_gather(values, ("ring", "depth"), axis=0, tiled=True)

    def scatter_half(self, values, *due):
        kept = lax.dynamic_index_in_dim(values, self.half, 0, keepdims=False)
        sent = lax.dynamic_index_in_dim(values, 1 - self.half, 0, keepdims=False)
        came = after(self.to_half(sent), *due)
        return (kept.astype(WIDE) + came.astype(WIDE)).astype(LOW)

    def scatter_teams(self, values):
        return lax.psum_scatter(
            values, ("half", "ring", "depth"), scatter_dimension=0, tiled=True
        )

    def scatter_rest(self, values):
        return lax.psum_scatter(values, ("ring", "depth"), scatter_dimension=0, tiled=True)

    def whole_columns(self, parts):
        parts = lax.all_to_all(parts, SQUARE, 0, 0, tiled=True)
        return parts.transpose(1, 0, 2).reshape(parts.shape[1], -1)

    def whole_rows(self, *packs):
        blocks = lax.axis_size(SQUARE)
        values = jnp.concatenate([pack for pack, _ in packs], axis=0)
        rows, columns = values.shape
        parts = values.reshape(rows, blocks, columns // blocks).transpose(1, 0, 2)
        parts = lax.all_to_all(parts, SQUARE, 0, 0, tiled=True)
        found, low = [], 0
        for pack, kinds in packs:
            share = pack.shape[0] // kinds
            part = parts[:, low : low + kinds * share].reshape(blocks, kinds, share, -1)
            found.append(part.transpose(1, 0, 2, 3).reshape(kinds, blocks * share, -1))
            low += kinds * share
        return found

    def gather_rows(self, values, *due):
        mate = self.to_rank(values, 1)
        across = after(self.to_rank(values, 2), *due)
        return [values, mate, across, self.to_rank(across, 1)]

    def scatter_rows(self, blocks, waiting=(), due=()):
        rows = blocks[0].shape[0]
        came = self.to_rank(jnp.concatenate([blocks[1], blocks[3]], axis=0).astype(LOW), 1)
        came, *waiting = lax.optimization_barrier((came, *waiting))
        across = (blocks[2].astype(WIDE) + came[rows:].astype(WIDE)).astype(LOW)
        own = blocks[0].astype(WIDE) + came[:rows].astype(WIDE)
        across = after(self.to_rank(across, 2), *due)
        return own + across.astype(WIDE), waiting

    def gather_square(self, values, *due):
        beside, opposite = self.to_rank(values, 2), self.to_half(values)
        rows = values.shape[0] // 2
        diagonal = jnp.concatenate(
            [self.to_half(beside[:rows]), self.to_rank(opposite[rows:], 2)], axis=0
        )
        diagonal = after(diagonal, *due)
        blocks = [values, beside, opposite, diagonal]
        return blocks + [self.to_rank(block, 1) for block in blocks]

    def scatter_square(self, values, waiting=(), due=()):
        size = values.shape[0] // 8
        rows = size // 2
        came = self.to_rank(values[4 * size :], 1)
        came, *waiting = lax.optimization_barrier((came, *waiting))
        sums = values[: 4 * size].astype(WIDE) + came.astype(WIDE)
        own, beside, opposite, diagonal = [sums[k * size : (k + 1) * size] for k in range(4)]
        diagonal = diagonal.astype(LOW)
        first = self.to_half(diagonal[:rows]).astype(WIDE)
        second = self.to_rank(diagonal[rows:], 2).astype(WIDE)
        beside = jnp.concatenate([beside[:rows] + first, beside[rows:]], axis=0).astype(LOW)
        opposite = jnp.concatenate([opposite[:rows], opposite[rows:] + second], axis=0).astype(LOW)
        beside, opposite = self.to_rank(beside, 2), self.to_half(opposite)
        beside = after(beside, *due)
        return own + beside.astype(WIDE) + opposite.astype(WIDE), waiting

    def total(self, values):
        sizes = (self.halves, 2, self.depth, self.rings, 2)
        for axis, size in enumerate(sizes):
            bit = 1
            while bit < size:
                values = values + self.move(
                    values, lambda *place: (*place[:axis], place[axis] ^ bit, *place[axis + 1 :])
                )
                bit *= 2
        return values


def after(values, *others):
    return lax.optimization_barrier((values, *others))[0] if others else values


def times(a, b):
    return lax.dot_general(a, b, (((1,), (0,)), ((), ())), preferred_element_type=WIDE)


def times_rows(a, b):
    return lax.dot_general(a, b, (((1,), (1,)), ((), ())), preferred_element_type=WIDE)


def columns_times(a, b):
    return lax.dot_general(a, b, (((0,), (0,)), ((), ())), preferred_element_type=WIDE)


def root_norm(values, gain_row):
    return (
        values * lax.rsqrt(jnp.mean(values * values, axis=-1, keepdims=True) + EPSILON) * gain_row
    )


def root_norm_back(inputs, gain_row, grad, arriving):
    widened = inputs.astype(WIDE)
    inverse = lax.rsqrt(jnp.mean(widened * widened, axis=-1, keepdims=True) + EPSILON)
    unit_rows = widened * inverse
    scaled = grad * gain_row
    through = inverse * (scaled - unit_rows * jnp.mean(scaled * unit_rows, axis=-1, keepdims=True))
    gain_grad = jnp.sum(grad * unit_rows, axis=0)
    return ((arriving.astype(WIDE) + through).astype(LOW), gain_grad)


def angles(offsets, head_width):
    inverse = ROTARY_BASE ** (-jnp.arange(0, head_width, 2).astype(WIDE) / head_width)
    phases = offsets.astype(WIDE)[:, None] * inverse[None, :]
    return (jnp.tile(jnp.cos(phases), (1, 4)), jnp.tile(jnp.sin(phases), (1, 4)))


def lanes(shape):
    return lax.broadcasted_iota(jnp.int32, shape, len(shape) - 1)


def pair_mean(values):
    width = values.shape[-1] // 2
    first = lanes(values.shape) < width
    low = jnp.sum(jnp.where(first, values, 0), axis=-1, keepdims=True)
    high = jnp.sum(jnp.where(first, 0, values), axis=-1, keepdims=True)
    return jnp.where(first, low, high) / width


def turned(values):
    width = values.shape[-1]
    quarter = width // 4
    ahead = pltpu.roll(values, width - quarter, 1)
    behind = pltpu.roll(values, quarter, 1)
    return jnp.where(lanes(values.shape) % (width // 2) < quarter, -ahead, behind)


def unit_pair(values):
    inverse = lax.rsqrt(pair_mean(values * values) + EPSILON)
    return values * inverse, inverse


def rotated(values, gain_row, cosine, sine):
    unit, _ = unit_pair(values)
    scaled = unit * gain_row
    return scaled * cosine + turned(scaled) * sine


def rotated_back(values, gain_row, cosine, sine, grad):
    unit, inverse = unit_pair(values)
    scaled_grad = grad * cosine - turned(grad * sine)
    unit_grad = scaled_grad * gain_row
    result = inverse * (unit_grad - unit * pair_mean(unit_grad * unit))
    return result, jnp.sum(scaled_grad * unit, axis=0, keepdims=True)


def heads_kernel(packed_ref, gains_ref, cosine_ref, sine_ref, queries_ref, pairs_ref):
    width = cosine_ref.shape[1]
    cosine, sine = cosine_ref[...], sine_ref[...]
    for g in range(packed_ref.shape[1] // (2 * width)):
        own = slice(g * width, (g + 1) * width)
        values = packed_ref[:, 2 * g * width : (2 * g + 1) * width]
        queries_ref[:, own] = rotated(values, gains_ref[0:1], cosine, sine).astype(LOW)
        values = packed_ref[:, (2 * g + 1) * width : (2 * g + 2) * width]
        keys = rotated(values, gains_ref[1:2], cosine, sine)
        first = lanes(values.shape) < width // 2
        pairs_ref[:, own] = jnp.where(first, keys, values).astype(LOW)


def heads_back_kernel(
    packed_ref, gains_ref, cosine_ref, sine_ref, queries_grad_ref, pairs_grad_ref, out_ref, gain_ref
):
    width = cosine_ref.shape[1]
    cosine, sine = cosine_ref[...], sine_ref[...]

    @pl.when(pl.program_id(0) == 0)
    def _():
        gain_ref[...] = jnp.zeros_like(gain_ref)

    for g in range(packed_ref.shape[1] // (2 * width)):
        own = slice(g * width, (g + 1) * width)
        for part, grad_ref in ((0, queries_grad_ref), (1, pairs_grad_ref)):
            place = slice((2 * g + part) * width, (2 * g + part + 1) * width)
            grad = grad_ref[:, own].astype(WIDE)
            result, gain_grad = rotated_back(
                packed_ref[:, place], gains_ref[part : part + 1], cosine, sine, grad
            )
            if part:
                result = jnp.where(lanes(result.shape) < width // 2, result, grad)
            out_ref[:, place] = result.astype(LOW)
            gain_ref[part : part + 1] += gain_grad


def split_heads(packed, gains, cosine, sine, rows):
    total, columns = packed.shape
    width = cosine.shape[1]
    row_block = lambda size: pl.BlockSpec((rows, size), lambda i: (i, 0))
    return pl.pallas_call(
        heads_kernel,
        grid=(total // rows,),
        in_specs=[
            row_block(columns),
            pl.BlockSpec((2, width), lambda i: (0, 0)),
            row_block(width),
            row_block(width),
        ],
        out_specs=[row_block(columns // 2), row_block(columns // 2)],
        out_shape=[jax.ShapeDtypeStruct((total, columns // 2), LOW)] * 2,
        compiler_params=pltpu.CompilerParams(vmem_limit_bytes=48 << 20),
        name="heads",
    )(packed, gains, cosine, sine)


def split_heads_back(packed, gains, cosine, sine, queries_grad, pairs_grad, rows):
    total, columns = packed.shape
    width = cosine.shape[1]
    row_block = lambda size: pl.BlockSpec((rows, size), lambda i: (i, 0))
    return pl.pallas_call(
        heads_back_kernel,
        grid=(total // rows,),
        in_specs=[
            row_block(columns),
            pl.BlockSpec((2, width), lambda i: (0, 0)),
            row_block(width),
            row_block(width),
            row_block(columns // 2),
            row_block(columns // 2),
        ],
        out_specs=[row_block(columns), pl.BlockSpec((2, width), lambda i: (0, 0))],
        out_shape=[
            jax.ShapeDtypeStruct((total, columns), LOW),
            jax.ShapeDtypeStruct((2, width), WIDE),
        ],
        compiler_params=pltpu.CompilerParams(vmem_limit_bytes=48 << 20),
        name="heads_back",
    )(packed, gains, cosine, sine, queries_grad, pairs_grad)


def block_weights(offsets, queries, keys, scale):
    scores = (
        lax.dot_general(queries, keys, (((1,), (1,)), ((), ())), preferred_element_type=WIDE)
        * scale
    )
    rows, window = offsets.shape[0], keys.shape[0]
    shape = (rows, window)
    back = (
        lax.broadcasted_iota(jnp.int32, shape, 0)
        + LONGEST
        - lax.broadcasted_iota(jnp.int32, shape, 1)
    )
    allowed = (back >= 0) & (back <= offsets)
    allowed = jnp.concatenate([allowed.astype(WIDE)] * (queries.shape[0] // rows), axis=0) > 0.5
    scores = jnp.where(allowed, scores, NEGATIVE)
    weights = jnp.exp(scores - jnp.max(scores, axis=-1, keepdims=True))
    return weights * (1 / jnp.sum(weights, axis=-1, keepdims=True))


def over(values):
    width = values.shape[1] // 2
    return jnp.concatenate([values[:, :width], values[:, width:]], axis=0)


def beside(values):
    rows = values.shape[0] // 2
    return jnp.concatenate([values[:rows], values[rows:]], axis=1)


def attend_kernel(scale, offsets_ref, queries_ref, pairs_ref, out_ref):
    rows, width = queries_ref.shape[0], queries_ref.shape[1] // 2
    low = pl.multiple_of(pl.program_id(1) * rows, rows)
    pairs = pairs_ref[pl.ds(low, LONGEST + rows), :]
    keys, values = pairs[:, :width], pairs[:, width:]
    shape = (rows, pairs.shape[0])
    back = (
        lax.broadcasted_iota(jnp.int32, shape, 0)
        + LONGEST
        - lax.broadcasted_iota(jnp.int32, shape, 1)
    )
    allowed = (back >= 0) & (back <= offsets_ref[...])
    results = []
    for head in range(2):
        queries = queries_ref[:, head * width : (head + 1) * width]
        scores = lax.dot_general(
            queries, keys, (((1,), (1,)), ((), ())), preferred_element_type=WIDE
        )
        scores = jnp.where(allowed, scores, NEGATIVE)
        weights = jnp.exp((scores - jnp.max(scores, axis=-1, keepdims=True)) * scale)
        weights = weights * (1 / jnp.sum(weights, axis=-1, keepdims=True))
        result = jnp.dot(weights.astype(LOW), values, preferred_element_type=WIDE)
        results.append(result.astype(LOW))
    out_ref[...] = jnp.concatenate(results, axis=1)


def attend_back_kernel(
    scale, offsets_ref, queries_ref, pairs_ref, grad_ref, queries_grad_ref, pairs_grad_ref
):
    rows, width = queries_ref.shape[0], queries_ref.shape[1] // 2

    @pl.when(pl.program_id(1) == 0)
    def _():
        pairs_grad_ref[...] = jnp.zeros_like(pairs_grad_ref)

    low = pl.multiple_of(pl.program_id(1) * rows, rows)
    window = pl.ds(low, LONGEST + rows)
    queries, grad = over(queries_ref[...]), over(grad_ref[...])
    pairs = pairs_ref[window, :]
    keys, values = pairs[:, :width], pairs[:, width:]
    weights = block_weights(offsets_ref[...], queries, keys, scale)
    flow = lax.dot_general(grad, values, (((1,), (1,)), ((), ())), preferred_element_type=WIDE)
    inner = jnp.sum(weights * flow, axis=-1, keepdims=True)
    score_grad = (weights * (flow - inner)).astype(LOW)
    values_grad = lax.dot_general(
        weights.astype(LOW), grad, (((0,), (0,)), ((), ())), preferred_element_type=WIDE
    )
    keys_grad = lax.dot_general(
        score_grad, queries, (((0,), (0,)), ((), ())), preferred_element_type=WIDE
    )
    pairs_grad_ref[window, :] += jnp.concatenate([keys_grad * scale, values_grad], axis=1)
    queries_grad = jnp.dot(score_grad, keys, preferred_element_type=WIDE) * scale
    queries_grad_ref[...] = beside(queries_grad.astype(LOW))


def attention_specs(queries, pairs, rows, head_width):
    width = 2 * head_width
    grid = (queries.shape[1] // width, queries.shape[0] // rows)
    offsets_spec = pl.BlockSpec((rows, 1), lambda g, i: (i, 0))
    rows_spec = pl.BlockSpec((rows, width), lambda g, i: (i, g))
    pairs_spec = pl.BlockSpec((pairs.shape[0], width), lambda g, i: (0, g))
    return (grid, offsets_spec, rows_spec, pairs_spec)


def attend(offsets, queries, pairs, rows, head_width):
    grid, offsets_spec, rows_spec, pairs_spec = attention_specs(queries, pairs, rows, head_width)
    return pl.pallas_call(
        functools.partial(attend_kernel, head_width ** (-0.5)),
        grid=grid,
        in_specs=[offsets_spec, rows_spec, pairs_spec],
        out_specs=rows_spec,
        out_shape=jax.ShapeDtypeStruct(queries.shape, LOW),
        compiler_params=pltpu.CompilerParams(vmem_limit_bytes=48 << 20),
        name="attend",
    )(offsets[:, None], queries, pairs)


def attend_back(offsets, queries, pairs, grad, rows, head_width):
    grid, offsets_spec, rows_spec, pairs_spec = attention_specs(queries, pairs, rows, head_width)
    return pl.pallas_call(
        functools.partial(attend_back_kernel, head_width ** (-0.5)),
        grid=grid,
        in_specs=[offsets_spec, rows_spec, pairs_spec, rows_spec],
        out_specs=[rows_spec, pairs_spec],
        out_shape=[
            jax.ShapeDtypeStruct(queries.shape, LOW),
            jax.ShapeDtypeStruct(pairs.shape, WIDE),
        ],
        compiler_params=pltpu.CompilerParams(vmem_limit_bytes=48 << 20),
        name="attend_back",
    )(offsets[:, None], queries, pairs, grad)


def whole_rows_of(ref):
    teams, rows, columns = ref.shape
    return ref[...].reshape(teams * rows, columns)


def dot_nt(a, b):
    return lax.dot_general(a, b, (((1,), (1,)), ((), ())), preferred_element_type=WIDE)


def feed_kernel(
    normed_ref, gate_ref, up_ref, outward_ref, gated_ref, raised_ref, hidden_ref, update_ref
):
    normed = normed_ref[...]
    gate = dot_nt(normed, whole_rows_of(gate_ref))
    up = dot_nt(normed, whole_rows_of(up_ref))
    gated_ref[...] = gate.astype(LOW)
    raised_ref[...] = up.astype(LOW)
    hidden = (gate / (1 + jnp.exp(-gate)) * up).astype(LOW)
    hidden_ref[...] = hidden
    update_ref[...] = jnp.dot(
        hidden, whole_rows_of(outward_ref), preferred_element_type=WIDE
    ).astype(LOW)


def feed_back_kernel(
    full_ref,
    gated_ref,
    raised_ref,
    gate_ref,
    up_ref,
    outward_ref,
    gate_grad_ref,
    up_grad_ref,
    update_ref,
    *turned_ref,
):
    if turned_ref:

        @pl.when(pl.program_id(0) == 0)
        def _():
            turned_ref[0][...] = whole_rows_of(outward_ref).T

        hidden_grad = jnp.dot(
            full_ref[...], turned_ref[0][...], preferred_element_type=WIDE
        )
    else:
        hidden_grad = dot_nt(full_ref[...], whole_rows_of(outward_ref))
    gate = gated_ref[...].astype(WIDE)
    up = raised_ref[...].astype(WIDE)
    sigmoid = 1 / (1 + jnp.exp(-gate))
    through = hidden_grad * sigmoid
    gate_grad = (through * up * (1 + gate * (1 - sigmoid))).astype(LOW)
    up_grad = (through * gate).astype(LOW)
    gate_grad_ref[...] = gate_grad
    up_grad_ref[...] = up_grad
    update = jnp.dot(gate_grad, whole_rows_of(gate_ref), preferred_element_type=WIDE)
    update += jnp.dot(up_grad, whole_rows_of(up_ref), preferred_element_type=WIDE)
    update_ref[...] = update.astype(LOW)


def feed_grads_kernel(
    gate_grad_ref, up_grad_ref, hidden_ref, normed_ref, full_ref, out_ref, total_ref
):
    teams, rows, columns = out_ref.shape
    width, step = teams * rows, 128

    def fill(left_ref, right_ref):
        for low in range(0, width, step):
            own = slice(low, min(low + step, width))
            total_ref[own] = lax.dot_general(
                left_ref[:, own],
                right_ref[...],
                (((0,), (0,)), ((), ())),
                preferred_element_type=WIDE,
            )
        out_ref[...] = total_ref[...].astype(LOW).reshape(teams, rows, columns)

    pl.when(pl.program_id(0) == 0)(lambda: fill(gate_grad_ref, normed_ref))
    pl.when(pl.program_id(0) == 1)(lambda: fill(up_grad_ref, normed_ref))
    pl.when(pl.program_id(0) == 2)(lambda: fill(hidden_ref, full_ref))


def kind_spec(pack, k):
    teams, _, rows, columns = pack.shape
    return pl.BlockSpec((teams, None, rows, columns), lambda i: (0, k, 0, 0))


def row_spec(rows, columns):
    return pl.BlockSpec((rows, columns), lambda i: (i, 0))


def feed_call(normed, pack, rows):
    total, columns = normed.shape
    width = pack.shape[0] * pack.shape[2]
    wide = jax.ShapeDtypeStruct((total, width), LOW)
    return pl.pallas_call(
        feed_kernel,
        grid=(total // rows,),
        in_specs=[row_spec(rows, columns)] + [kind_spec(pack, k) for k in range(3)],
        out_specs=[row_spec(rows, width)] * 3 + [row_spec(rows, columns)],
        out_shape=[wide] * 3 + [jax.ShapeDtypeStruct((total, columns), LOW)],
        compiler_params=pltpu.CompilerParams(vmem_limit_bytes=48 << 20),
        name="feed",
    )(normed, pack, pack, pack)


def feed_back_call(full, gated, raised, pack, rows, turned):
    total, columns = full.shape
    width = gated.shape[1]
    wide = jax.ShapeDtypeStruct((total, width), LOW)
    return pl.pallas_call(
        feed_back_kernel,
        grid=(total // rows,),
        in_specs=[row_spec(rows, columns)]
        + [row_spec(rows, width)] * 2
        + [kind_spec(pack, k) for k in range(3)],
        out_specs=[row_spec(rows, width)] * 2 + [row_spec(rows, columns)],
        out_shape=[wide] * 2 + [jax.ShapeDtypeStruct((total, columns), LOW)],
        scratch_shapes=[pltpu.VMEM((columns, width), LOW)] if turned else [],
        compiler_params=pltpu.CompilerParams(vmem_limit_bytes=48 << 20),
        name="feed_back",
    )(full, gated, raised, pack, pack, pack)


def feed_grads_call(gate_grad, up_grad, hidden, normed, full, teams):
    total, columns = normed.shape
    width = hidden.shape[1]
    wide_spec = pl.BlockSpec((total, width), lambda k: (0, 0))
    rows_spec = pl.BlockSpec((total, columns), lambda k: (0, 0))
    return pl.pallas_call(
        feed_grads_kernel,
        grid=(3,),
        in_specs=[wide_spec] * 3 + [rows_spec] * 2,
        out_specs=pl.BlockSpec((teams, None, width // teams, columns), lambda k: (0, k, 0, 0)),
        out_shape=jax.ShapeDtypeStruct((teams, 3, width // teams, columns), LOW),
        scratch_shapes=[pltpu.VMEM((width, columns), WIDE)],
        compiler_params=pltpu.CompilerParams(vmem_limit_bytes=58 << 20),
        name="feed_grads",
    )(gate_grad, up_grad, hidden, normed, full)


def local(
    tokens,
    lengths,
    gains,
    qk_gains,
    conv_kernel,
    conv_in,
    conv_out,
    ffn1_in,
    ffn1_out,
    attn_qkv,
    attn_out,
    ffn2_in,
    ffn2_out,
    cotangent,
):
    here = Place()
    depth = here.depth
    stretch = tokens.shape[1]
    slice_width = tokens.shape[2]
    model_width = slice_width * depth
    sections = 2 * here.halves
    stream_rows = sections * stretch
    team_rows = stream_rows // depth
    own_rows = team_rows // RANKS
    head_width = attn_qkv.shape[2] // 4
    groups_here = attn_qkv.shape[1]
    groups = groups_here * depth // RANKS
    block_width = conv_in.shape[0]
    query_rows = min(256, team_rows)
    feed_block = min(512, team_rows)
    spare = depth // RANKS

    def row_goal(k):
        def goal(half, side, z, ring, core):
            part = (z + k) % depth
            rank = part % RANKS
            batch = half * 2 + side
            return (core, rank // 2, batch * spare + part // RANKS, ring, rank % 2)

        return goal

    own_part = (here.z % spare) * RANKS + here.rank

    def row_pieces(values):
        grid = values.reshape(depth, own_rows, slice_width)
        return [
            here.move(
                lax.dynamic_index_in_dim(grid, (here.z + k) % depth, 0, keepdims=False),
                row_goal(k),
            )
            for k in range(depth)
        ]

    def rows_in(pieces):
        columns = here.mirrored(jnp.stack(lax.optimization_barrier(tuple(pieces))), own_part)
        return columns.transpose(1, 0, 2).reshape(own_rows, model_width)

    def rows_out(*arrays):
        count = len(arrays)
        grid = jnp.concatenate(arrays, axis=0).reshape(count * own_rows, depth, slice_width)
        grid = grid.transpose(1, 0, 2)
        pieces = []
        for k in range(depth):
            piece = lax.dynamic_index_in_dim(grid, (own_part - k) % depth, 0, keepdims=False)
            route = [(goal, source) for source, goal in here.route(row_goal(k))]
            pieces.append(lax.ppermute(piece, AXES, route))
        rows = here.rolled(jnp.stack(pieces), here.z)
        rows = rows.reshape(depth, count, own_rows, slice_width).transpose(1, 0, 2, 3)
        return list(rows.reshape(count, 1, stretch, slice_width))

    def inward(values):
        return values.transpose(1, 2, 0)

    def by_square(values):
        kinds, rows, columns = values.shape
        blocks = lax.axis_size(SQUARE)
        parts = values.reshape(kinds, blocks, rows // blocks, columns).transpose(1, 0, 2, 3)
        return parts.reshape(blocks, kinds * (rows // blocks), columns)

    rest = here.rings * depth
    teams = here.halves * rest

    def split_kinds(values, kinds):
        grid = values.reshape(here.halves, rest, kinds, -1, model_width)
        return [grid[:, :, k].reshape(-1, model_width) for k in range(kinds)]

    def halves_sum(grads, *due):
        grids = [grad.astype(LOW).reshape(here.halves, rest, -1, model_width) for grad in grads]
        return here.scatter_half(
            jnp.concatenate(grids, axis=2).reshape(here.halves, -1, model_width), *due
        )

    taps = conv_kernel.shape[0]
    square = lax.axis_index(SQUARE)
    share = slice_width // lax.axis_size(SQUARE)
    channels = teams * share

    heads_rows = attn_out.shape[0] // groups_here
    heads_size = attn_qkv.shape[2] + heads_rows

    def heads_goal(half, side, z, ring, core):
        rank = z // spare
        return (half, rank // 2, (2 * side + core) * spare + z % spare, ring, rank % 2)

    heads_part = jnp.concatenate(
        [inward(attn_qkv), attn_out.reshape(groups_here, heads_rows, -1)], axis=1
    )
    heads_flat = heads_part.shape[0] * heads_part.shape[1]
    heads_moved = here.move(heads_part.reshape(heads_flat, block_width), heads_goal)

    def heads_unpack(gathered):
        blocks = gathered.reshape(
            here.halves, here.rings, 2, 2, spare, groups_here * heads_size, block_width
        )
        ordered = [
            blocks[half, ring, side, core].reshape(groups * heads_size, block_width)
            for half in range(here.halves)
            for side in range(2)
            for ring in range(here.rings)
            for core in range(2)
        ]
        weights = jnp.concatenate(ordered, axis=1).reshape(groups, heads_size, model_width)
        return (
            weights[:, : heads_size - heads_rows].reshape(-1, model_width),
            weights[:, heads_size - heads_rows :].reshape(-1, model_width),
        )

    def heads_rows_of(inward_grad, outward_grad):
        grad = jnp.concatenate(
            [
                inward_grad.astype(LOW).reshape(groups, -1, model_width),
                outward_grad.astype(LOW).reshape(groups, -1, model_width),
            ],
            axis=1,
        ).reshape(groups * heads_size, model_width)
        blocks = [
            grad[:, block_width * k : block_width * (k + 1)]
            for k in range(model_width // block_width)
        ]
        ordered = [
            blocks[((half * 2 + side) * here.rings + ring) * 2 + core]
            for half in range(here.halves)
            for ring in range(here.rings)
            for side in range(2)
            for core in range(2)
        ]
        return jnp.concatenate(ordered, axis=0)

    mixer_flat = 4 * share
    feed_rows = 3 * ffn1_out.shape[0] // lax.axis_size(SQUARE)
    mixer_whole = here.whole_columns(
        by_square(jnp.concatenate([inward(conv_in), conv_out[None]], axis=0))
    )
    residual = rows_in(row_pieces(after(tokens, mixer_whole)))
    own_taps = lax.dynamic_slice_in_dim(conv_kernel, square * share, share, 1)
    own_taps = jnp.pad(own_taps, ((0, 16 - taps), (0, model_width - share)))
    mixer_teams = here.gather_teams(jnp.concatenate([mixer_whole, own_taps], axis=0))
    feed_packs = [
        by_square(jnp.concatenate([inward(inner), outer[None]], axis=0))
        for inner, outer in ((ffn1_in, ffn1_out), (ffn2_in, ffn2_out))
    ]
    feed_parts = here.whole_columns(after(jnp.concatenate(feed_packs, axis=1), mixer_whole))
    mixer_part = mixer_teams.reshape(here.halves, rest, -1, model_width)
    mixer_weights = jnp.concatenate(
        split_kinds(mixer_part[:, :, :mixer_flat].reshape(-1, model_width), 4), axis=0
    )
    mixer_inward, mixer_outward = mixer_weights[: 3 * channels], mixer_weights[3 * channels :]
    kernel = (
        mixer_part[:, :, mixer_flat : mixer_flat + taps, :share]
        .transpose(2, 0, 1, 3)
        .reshape(taps, channels)
        .astype(WIDE)
    )

    aligned = feed_rows % 48 == 0
    out_rows = feed_rows // 3

    def feed_pack(gathered):
        pack = gathered.reshape(-1, 3, out_rows, model_width)
        if aligned:
            return pack
        return pack.transpose(1, 0, 2, 3).reshape(1, 3, -1, model_width)

    def feed_teams_of(grad):
        if not aligned:
            grad = grad.reshape(3, -1, out_rows, model_width).transpose(1, 0, 2, 3)
        return grad.reshape(-1, model_width)

    first_rest = here.gather_rest(after(feed_parts[:feed_rows], mixer_teams, residual))
    first_pack = feed_pack(first_rest)

    own_lengths = jnp.where(here.half == here.core, lengths[0], here.to_rank(lengths[0], 1))
    places = here.z * team_rows + jnp.arange(team_rows + 2, dtype=jnp.int32)
    passed = (places[:, None] >= jnp.cumsum(own_lengths)[None, :]).astype(jnp.int32)
    offsets = places - jnp.sum(passed * own_lengths[None, :], axis=1)
    first_mask = (offsets >= 1).astype(WIDE)[:, None]
    second_mask = (offsets >= 2).astype(WIDE)[:, None]
    offsets = offsets[:team_rows]
    cosine_rows, sine_rows = angles(offsets, head_width)
    beside_gains = here.to_rank(gains, 2)
    half_gains = jnp.where(
        here.side == 0,
        jnp.concatenate([gains, beside_gains]),
        jnp.concatenate([beside_gains, gains]),
    )
    all_gains = half_gains
    if here.halves > 1:
        other_gains = here.to_half(half_gains)
        all_gains = jnp.where(
            here.half == 0,
            jnp.concatenate([half_gains, other_gains]),
            jnp.concatenate([other_gains, half_gains]),
        )
    pair_gains = jnp.tile(qk_gains, (1, 2))

    def gather_ordered(values, *due):
        return jnp.concatenate(here.by_rank(here.gather_rows(values, *due)), axis=0)

    def gather_any(values, *due):
        return jnp.concatenate(here.gather_rows(values, *due), axis=0)

    def scatter_ordered(values, waiting=(), due=()):
        grid = values.astype(LOW).reshape(RANKS, own_rows, model_width)
        blocks = [
            lax.dynamic_index_in_dim(grid, jnp.bitwise_xor(here.rank, k), 0, keepdims=False)
            for k in range(RANKS)
        ]
        return here.scatter_rows(blocks, waiting, due)

    def scatter_any(values, waiting=(), due=()):
        grid = values.astype(LOW).reshape(RANKS, own_rows, model_width)
        return here.scatter_rows([grid[k] for k in range(RANKS)], waiting, due)

    def joined(residual, update):
        return (residual.astype(WIDE) + update).astype(LOW)

    def mixer_forward(residual):
        normed = gather_ordered(root_norm(residual.astype(WIDE), all_gains[0]).astype(LOW))
        projected = times_rows(normed, mixer_inward)
        before, gate, behind = (
            projected[:, :channels],
            projected[:, channels : 2 * channels],
            projected[:, 2 * channels :],
        )
        product = before * behind
        tail = here.up(product[-2:], 1)
        extended = jnp.concatenate([tail, product], axis=0)
        once = extended[1:-1] * first_mask[:team_rows]
        twice = extended[:-2] * second_mask[:team_rows]
        mixed = kernel[2] * product + kernel[1] * once + kernel[0] * twice
        gated = (gate * mixed).astype(LOW)
        update, _ = scatter_ordered(times(gated, mixer_outward))
        return joined(residual, update), (
            residual, normed, before, gate, behind, product, once, twice, mixed, gated,
        )

    def mixer_backward(arriving, saved, *due):
        residual, normed, before, gate, behind, product, once, twice, mixed, gated = saved
        full = gather_ordered(arriving, *due)
        gated_grad = times_rows(full, mixer_outward)
        gate_grad = gated_grad * mixed
        mixed_grad = gated_grad * gate
        following = here.up(mixed_grad[:2], -1)
        extended = jnp.concatenate([mixed_grad, following], axis=0)
        product_grad = (
            kernel[2] * mixed_grad
            + kernel[1] * extended[1:-1] * first_mask[1:-1]
            + kernel[0] * extended[2:] * second_mask[2:]
        )
        kernel_grad = jnp.stack(
            [
                jnp.sum(mixed_grad * twice, axis=0),
                jnp.sum(mixed_grad * once, axis=0),
                jnp.sum(mixed_grad * product, axis=0),
            ]
        )
        low = jnp.concatenate(
            [product_grad * behind, gate_grad, product_grad * before], axis=1
        ).astype(LOW)
        update, (low, full) = scatter_ordered(times(low, mixer_inward), (low, full))
        grad = [columns_times(low[:, k * channels : (k + 1) * channels], normed) for k in range(3)]
        grad.append(columns_times(gated, full))
        leaving, gain_grad = root_norm_back(residual, all_gains[0], update, arriving)
        return leaving, gain_grad, kernel_grad, grad, low

    def square_rows(values, *due):
        return jnp.concatenate(here.gather_square(values, *due), axis=0)

    def square_sums(values, waiting=(), due=()):
        return here.scatter_square(values.astype(LOW), waiting, due)

    def feed_forward(residual, gain_row, pack, gather, *due):
        normed = gather(root_norm(residual.astype(WIDE), gain_row).astype(LOW), *due)
        gated, raised, hidden, update = feed_call(normed, pack, feed_block)
        return update, (residual, normed, gated, raised, hidden)

    def feed_joined(residual, update, scatter, due=()):
        return joined(residual, scatter(update, (), due)[0])

    def feed_backward(arriving, saved, gain_row, pack, gather, scatter, *due):
        residual, normed, gated, raised, hidden = saved
        full = gather(arriving, *due)
        square = full.shape[0] > team_rows
        gate_grad, up_grad, update = feed_back_call(
            full, gated, raised, pack, query_rows if square else feed_block, square
        )
        update, (gate_grad, up_grad, full) = scatter(update, (gate_grad, up_grad, full))
        grad = feed_grads_call(gate_grad, up_grad, hidden, normed, full, pack.shape[0])
        update = after(update, grad)
        leaving, gain_grad = root_norm_back(residual, gain_row, update, arriving)
        return leaving, gain_grad, feed_teams_of(grad)

    halo_steps = LONGEST // team_rows

    def heads_forward(residual, due):
        normed = root_norm(residual.astype(WIDE), all_gains[2]).astype(LOW)
        normed = gather_ordered(normed, *due[0])
        packed = times_rows(normed, heads_inward)
        queries, pairs = split_heads(packed, pair_gains, cosine_rows, sine_rows, query_rows)
        window = jnp.concatenate(
            [here.up(pairs, step) for step in range(halo_steps, 0, -1)] + [pairs], axis=0
        )
        window = after(window, *due[1])
        attended = attend(offsets, queries, window, query_rows, head_width)
        update, _ = scatter_ordered(times(attended, heads_outward), (), due[2])
        return joined(residual, update), (residual, normed, packed, queries, window, attended)

    def heads_backward(arriving, saved):
        residual, normed, packed, queries, window, attended = saved
        full = gather_ordered(arriving)
        attended_grad = times_rows(full, heads_outward).astype(LOW)
        queries_grad, pairs_grad = attend_back(
            offsets, queries, window, attended_grad, query_rows, head_width
        )
        own = pairs_grad[LONGEST:]
        for step in range(1, halo_steps + 1):
            low = (halo_steps - step) * team_rows
            moved = here.up(pairs_grad[low : low + team_rows].astype(LOW), -step)
            own = own + moved.astype(WIDE)
        own = own.astype(LOW)
        low, pair_gains_grad = split_heads_back(
            packed, pair_gains, cosine_rows, sine_rows, queries_grad, own, query_rows
        )
        update, (low, full) = scatter_ordered(times(low, heads_inward), (low, full))
        inward_grad = columns_times(low, normed)
        outward_grad = columns_times(attended, full)
        leaving, gain_grad = root_norm_back(residual, all_gains[2], update, arriving)
        width = head_width
        head_gains_grad = jnp.stack(
            [pair_gains_grad[0, :width] + pair_gains_grad[0, width:], pair_gains_grad[1, :width]]
        )
        return leaving, gain_grad, head_gains_grad, inward_grad, outward_grad, own

    residual, mixer_saved = mixer_forward(residual)
    heads_teams = here.gather_teams(after(heads_moved, first_rest, residual))
    heads_inward, heads_outward = heads_unpack(heads_teams)
    update, first_saved = feed_forward(residual, all_gains[1], first_pack, square_rows)
    residual = feed_joined(residual, update, square_sums)
    second_teams = here.gather_teams(after(feed_parts[feed_rows:], heads_teams, update))
    second_pack = feed_pack(second_teams)
    pieces = row_pieces(after(cotangent, residual))
    residual, heads_saved = heads_forward(
        residual, [(heads_inward, heads_outward, *pieces[:1]), pieces[1:2], pieces[2:3]]
    )
    last_update, second_saved = feed_forward(
        residual, all_gains[3], second_pack, gather_any, *pieces[3:]
    )
    flowing = rows_in(pieces)

    flowing, gain3, second_grad = feed_backward(
        flowing, second_saved, all_gains[3], second_pack, gather_any, scatter_any
    )
    flowing, gain2, head_gains_grad, heads_inward_grad, heads_outward_grad, pairs_low = (
        heads_backward(flowing, heads_saved)
    )
    second_sum = here.scatter_teams(after(second_grad, pairs_low))
    output = feed_joined(residual, after(last_update, flowing), scatter_any)
    heads_grad = heads_rows_of(heads_inward_grad, heads_outward_grad)
    heads_half = here.scatter_half(heads_grad.reshape(here.halves, -1, block_width))
    flowing, gain1, first_grad = feed_backward(
        flowing,
        first_saved,
        all_gains[1],
        first_pack,
        square_rows,
        square_sums,
        heads_grad,
    )
    first_sum = here.scatter_rest(after(first_grad, flowing, second_sum))
    flowing, gain0, kernel_grad, mixer_grad, low = mixer_backward(
        flowing, mixer_saved, output
    )
    mixer_half = halves_sum([mixer_grad[k] for k in range(4)])
    output, input_grad = rows_out(output, after(flowing, mixer_half))
    late = [part.reshape(rest, -1, model_width) for part in (heads_half, mixer_half)]
    late_sum = here.scatter_rest(
        after(jnp.concatenate(late, axis=1).reshape(-1, model_width), first_sum)
    )

    heads_route = [(b, a) for a, b in here.route(heads_goal)]
    (second_grad,) = here.whole_rows((after(second_sum, input_grad), 3))
    (first_grad,) = here.whole_rows((after(first_sum, second_grad), 3))
    heads_wide = heads_flat * block_width // model_width
    heads_grad = late_sum[:heads_wide].reshape(heads_flat, block_width)
    heads_grad = lax.ppermute(heads_grad, AXES, heads_route).reshape(heads_part.shape)
    (mixer_grad,) = here.whole_rows((late_sum[heads_wide:], 4))

    def outside(values):
        return values.transpose(2, 0, 1).astype(WIDE)

    kernel_blocks = kernel_grad.reshape(taps, here.halves, 1, here.rings, depth, 1, share)
    sides = (jnp.arange(2) == here.side).astype(WIDE).reshape(2, 1, 1, 1, 1)
    cores = (jnp.arange(2) == here.core).astype(WIDE).reshape(2, 1)
    kernel_whole = (kernel_blocks * sides * cores).transpose(0, 4, 1, 2, 3, 5, 6)
    small = jnp.concatenate(
        [
            jnp.stack([gain0, gain1, gain2, gain3]).reshape(-1),
            kernel_whole.reshape(-1),
            head_gains_grad.reshape(-1),
        ]
    )
    small = here.total(after(small, input_grad))
    gain_size, kernel_size = 4 * model_width, taps * model_width
    return (
        output,
        input_grad,
        small[:gain_size].reshape(4, model_width),
        small[gain_size + kernel_size :].reshape(2, head_width),
        small[gain_size : gain_size + kernel_size].reshape(taps, model_width),
        outside(mixer_grad[:3]),
        mixer_grad[3].astype(WIDE),
        outside(first_grad[:2]),
        first_grad[2].astype(WIDE),
        outside(heads_grad[:, : heads_size - heads_rows]),
        heads_grad[:, heads_size - heads_rows :].reshape(attn_out.shape).astype(WIDE),
        outside(second_grad[:2]),
        second_grad[2].astype(WIDE),
    )


def solution(mesh):
    sections, depth, replicas = mesh.devices.shape
    fine = Mesh(mesh.devices.reshape(sections // 2, 2, depth, replicas // 2, 2), AXES)
    rows = P(SQUARE, None, "depth")
    columns = P("depth", SQUARE)
    heads = P(SQUARE, "depth", None)
    stream = P(("half", "side"), ("ring", "core"), "depth")
    return jax.shard_map(
        local,
        mesh=fine,
        in_specs=(
            stream,
            P(("ring", "core"), None),
            P(("half", "side"), None),
            P(),
            P(None, "depth"),
            rows,
            columns,
            rows,
            columns,
            heads,
            columns,
            rows,
            columns,
            stream,
        ),
        out_specs=(
            stream,
            stream,
            P(),
            P(),
            P(),
            rows,
            columns,
            rows,
            columns,
            heads,
            columns,
            rows,
            columns,
        ),
        check_vma=False,
    )
```

```python
import functools

import jax
import jax.numpy as jnp
from jax import lax
from jax.experimental import pallas as pl
from jax.experimental.pallas import tpu as pltpu
from jax.sharding import Mesh
from jax.sharding import PartitionSpec as P

EPSILON = 1e-05
ROTARY_BASE = 1000000.0
NEGATIVE = -1e30
AXES = ("half", "side", "depth", "ring", "core")
SQUARE = ("half", "side", "ring", "core")
LOW = jnp.bfloat16
WIDE = jnp.float32
RANKS = 4
LONGEST = 1024


class Place:
    def __init__(self):
        self.halves = lax.axis_size("half")
        self.depth = lax.axis_size("depth")
        self.rings = lax.axis_size("ring")
        self.half = lax.axis_index("half")
        self.side = lax.axis_index("side")
        self.z = lax.axis_index("depth")
        self.ring = lax.axis_index("ring")
        self.core = lax.axis_index("core")
        self.rank = 2 * self.side + self.core

    def places(self):
        return [
            (half, side, z, ring, core)
            for half in range(self.halves)
            for side in range(2)
            for z in range(self.depth)
            for ring in range(self.rings)
            for core in range(2)
        ]

    def flat(self, half, side, z, ring, core):
        return (((half * 2 + side) * self.depth + z) * self.rings + ring) * 2 + core

    def route(self, target):
        pairs = [(place, target(*place)) for place in self.places()]
        return [(self.flat(*a), self.flat(*b)) for a, b in pairs if b is not None]

    def move(self, values, target):
        return lax.ppermute(values, AXES, self.route(target))

    def to_rank(self, values, k):
        return self.move(
            values, lambda half, side, z, ring, core: (half, side ^ (k >> 1), z, ring, core ^ (k & 1))
        )

    def up(self, values, distance=1):
        return self.move(
            values,
            lambda half, side, z, ring, core: (half, side, z + distance, ring, core)
            if 0 <= z + distance < self.depth
            else None,
        )

    def by_rank(self, blocks):
        return [
            lax.select_n(jnp.bitwise_xor(self.rank, b), *blocks) for b in range(RANKS)
        ]

    def mirrored(self, stacked, place):
        count = stacked.shape[0]
        flipped = jnp.concatenate([stacked[:1], stacked[:0:-1]], axis=0)
        return lax.dynamic_slice_in_dim(
            jnp.concatenate([flipped, flipped], axis=0), count - place, count, 0
        )

    def rolled(self, stacked, place):
        count = stacked.shape[0]
        return lax.dynamic_slice_in_dim(
            jnp.concatenate([stacked, stacked], axis=0), count - place, count, 0
        )

    def to_half(self, values):
        return self.move(
            values, lambda half, side, z, ring, core: (1 - half, side, z, ring, core)
        )

    def gather_teams(self, values):
        return lax.all_gather(values, ("half", "ring", "depth"), axis=0, tiled=True)

    def gather_rest(self, values):
        return lax.all_gather(values, ("ring", "depth"), axis=0, tiled=True)

    def scatter_half(self, values, *due):
        kept = lax.dynamic_index_in_dim(values, self.half, 0, keepdims=False)
        sent = lax.dynamic_index_in_dim(values, 1 - self.half, 0, keepdims=False)
        came = after(self.to_half(sent), *due)
        return (kept.astype(WIDE) + came.astype(WIDE)).astype(LOW)

    def scatter_teams(self, values):
        return lax.psum_scatter(
            values, ("half", "ring", "depth"), scatter_dimension=0, tiled=True
        )

    def scatter_rest(self, values):
        return lax.psum_scatter(values, ("ring", "depth"), scatter_dimension=0, tiled=True)

    def whole_columns(self, parts):
        parts = lax.all_to_all(parts, SQUARE, 0, 0, tiled=True)
        return parts.transpose(1, 0, 2).reshape(parts.shape[1], -1)

    def whole_rows(self, *packs):
        blocks = lax.axis_size(SQUARE)
        values = jnp.concatenate([pack for pack, _ in packs], axis=0)
        rows, columns = values.shape
        parts = values.reshape(rows, blocks, columns // blocks).transpose(1, 0, 2)
        parts = lax.all_to_all(parts, SQUARE, 0, 0, tiled=True)
        found, low = [], 0
        for pack, kinds in packs:
            share = pack.shape[0] // kinds
            part = parts[:, low : low + kinds * share].reshape(blocks, kinds, share, -1)
            found.append(part.transpose(1, 0, 2, 3).reshape(kinds, blocks * share, -1))
            low += kinds * share
        return found

    def gather_rows(self, values, *due):
        mate = self.to_rank(values, 1)
        across = after(self.to_rank(values, 2), *due)
        return [values, mate, across, self.to_rank(across, 1)]

    def scatter_rows(self, blocks, waiting=(), due=()):
        rows = blocks[0].shape[0]
        came = self.to_rank(jnp.concatenate([blocks[1], blocks[3]], axis=0).astype(LOW), 1)
        came, *waiting = lax.optimization_barrier((came, *waiting))
        across = (blocks[2].astype(WIDE) + came[rows:].astype(WIDE)).astype(LOW)
        own = blocks[0].astype(WIDE) + came[:rows].astype(WIDE)
        across = after(self.to_rank(across, 2), *due)
        return own + across.astype(WIDE), waiting

    def gather_square(self, values, *due):
        beside, opposite = self.to_rank(values, 2), self.to_half(values)
        rows = values.shape[0] // 2
        diagonal = jnp.concatenate(
            [self.to_half(beside[:rows]), self.to_rank(opposite[rows:], 2)], axis=0
        )
        diagonal = after(diagonal, *due)
        blocks = [values, beside, opposite, diagonal]
        return blocks + [self.to_rank(block, 1) for block in blocks]

    def scatter_square(self, values, waiting=(), due=()):
        size = values.shape[0] // 8
        rows = size // 2
        came = self.to_rank(values[4 * size :], 1)
        came, *waiting = lax.optimization_barrier((came, *waiting))
        sums = values[: 4 * size].astype(WIDE) + came.astype(WIDE)
        own, beside, opposite, diagonal = [sums[k * size : (k + 1) * size] for k in range(4)]
        diagonal = diagonal.astype(LOW)
        first = self.to_half(diagonal[:rows]).astype(WIDE)
        second = self.to_rank(diagonal[rows:], 2).astype(WIDE)
        beside = jnp.concatenate([beside[:rows] + first, beside[rows:]], axis=0).astype(LOW)
        opposite = jnp.concatenate([opposite[:rows], opposite[rows:] + second], axis=0).astype(LOW)
        beside, opposite = self.to_rank(beside, 2), self.to_half(opposite)
        beside = after(beside, *due)
        return own + beside.astype(WIDE) + opposite.astype(WIDE), waiting

    def total(self, values):
        sizes = (self.halves, 2, self.depth, self.rings, 2)
        bits = [
            (axis, 1 << power)
            for axis, size in enumerate(sizes)
            for power in range(size.bit_length() - 1)
        ]

        def moved(values, flips):
            def goal(*place):
                place = list(place)
                for axis, bit in flips:
                    place[axis] ^= bit
                return tuple(place)

            return self.move(values, goal)

        for k in range(0, len(bits), 2):
            own = values + moved(values, bits[k : k + 1])
            if k + 1 < len(bits):
                own = own + (moved(values, bits[k + 1 : k + 2]) + moved(values, bits[k : k + 2]))
            values = own
        return values


def after(values, *others):
    return lax.optimization_barrier((values, *others))[0] if others else values


def times(a, b):
    return lax.dot_general(a, b, (((1,), (0,)), ((), ())), preferred_element_type=WIDE)


def times_rows(a, b):
    return lax.dot_general(a, b, (((1,), (1,)), ((), ())), preferred_element_type=WIDE)


def columns_times(a, b):
    return lax.dot_general(a, b, (((0,), (0,)), ((), ())), preferred_element_type=WIDE)


def root_norm(values, gain_row):
    return (
        values * lax.rsqrt(jnp.mean(values * values, axis=-1, keepdims=True) + EPSILON) * gain_row
    )


def root_norm_back(inputs, gain_row, grad, arriving):
    widened = inputs.astype(WIDE)
    inverse = lax.rsqrt(jnp.mean(widened * widened, axis=-1, keepdims=True) + EPSILON)
    unit_rows = widened * inverse
    scaled = grad * gain_row
    through = inverse * (scaled - unit_rows * jnp.mean(scaled * unit_rows, axis=-1, keepdims=True))
    gain_grad = jnp.sum(grad * unit_rows, axis=0)
    return ((arriving.astype(WIDE) + through).astype(LOW), gain_grad)


def angles(offsets, head_width):
    inverse = ROTARY_BASE ** (-jnp.arange(0, head_width, 2).astype(WIDE) / head_width)
    phases = offsets.astype(WIDE)[:, None] * inverse[None, :]
    return (jnp.tile(jnp.cos(phases), (1, 4)), jnp.tile(jnp.sin(phases), (1, 4)))


def lanes(shape):
    return lax.broadcasted_iota(jnp.int32, shape, len(shape) - 1)


def pair_mean(values):
    width = values.shape[-1] // 2
    first = lanes(values.shape) < width
    low = jnp.sum(jnp.where(first, values, 0), axis=-1, keepdims=True)
    high = jnp.sum(jnp.where(first, 0, values), axis=-1, keepdims=True)
    return jnp.where(first, low, high) / width


def turned(values):
    width = values.shape[-1]
    quarter = width // 4
    ahead = pltpu.roll(values, width - quarter, 1)
    behind = pltpu.roll(values, quarter, 1)
    return jnp.where(lanes(values.shape) % (width // 2) < quarter, -ahead, behind)


def unit_pair(values):
    inverse = lax.rsqrt(pair_mean(values * values) + EPSILON)
    return values * inverse, inverse


def rotated(values, gain_row, cosine, sine):
    unit, _ = unit_pair(values)
    scaled = unit * gain_row
    return scaled * cosine + turned(scaled) * sine


def rotated_back(values, gain_row, cosine, sine, grad):
    unit, inverse = unit_pair(values)
    scaled_grad = grad * cosine - turned(grad * sine)
    unit_grad = scaled_grad * gain_row
    result = inverse * (unit_grad - unit * pair_mean(unit_grad * unit))
    return result, jnp.sum(scaled_grad * unit, axis=0, keepdims=True)


def heads_kernel(packed_ref, gains_ref, cosine_ref, sine_ref, queries_ref, pairs_ref):
    width = cosine_ref.shape[1]
    cosine, sine = cosine_ref[...], sine_ref[...]
    for g in range(packed_ref.shape[1] // (2 * width)):
        own = slice(g * width, (g + 1) * width)
        values = packed_ref[:, 2 * g * width : (2 * g + 1) * width]
        queries_ref[:, own] = rotated(values, gains_ref[0:1], cosine, sine).astype(LOW)
        values = packed_ref[:, (2 * g + 1) * width : (2 * g + 2) * width]
        keys = rotated(values, gains_ref[1:2], cosine, sine)
        first = lanes(values.shape) < width // 2
        pairs_ref[:, own] = jnp.where(first, keys, values).astype(LOW)


def heads_back_kernel(
    packed_ref, gains_ref, cosine_ref, sine_ref, queries_grad_ref, pairs_grad_ref, out_ref, gain_ref
):
    width = cosine_ref.shape[1]
    cosine, sine = cosine_ref[...], sine_ref[...]

    @pl.when(pl.program_id(0) == 0)
    def _():
        gain_ref[...] = jnp.zeros_like(gain_ref)

    for g in range(packed_ref.shape[1] // (2 * width)):
        own = slice(g * width, (g + 1) * width)
        for part, grad_ref in ((0, queries_grad_ref), (1, pairs_grad_ref)):
            place = slice((2 * g + part) * width, (2 * g + part + 1) * width)
            grad = grad_ref[:, own].astype(WIDE)
            result, gain_grad = rotated_back(
                packed_ref[:, place], gains_ref[part : part + 1], cosine, sine, grad
            )
            if part:
                result = jnp.where(lanes(result.shape) < width // 2, result, grad)
            out_ref[:, place] = result.astype(LOW)
            gain_ref[part : part + 1] += gain_grad


def split_heads(packed, gains, cosine, sine, rows):
    total, columns = packed.shape
    width = cosine.shape[1]
    row_block = lambda size: pl.BlockSpec((rows, size), lambda i: (i, 0))
    return pl.pallas_call(
        heads_kernel,
        grid=(total // rows,),
        in_specs=[
            row_block(columns),
            pl.BlockSpec((2, width), lambda i: (0, 0)),
            row_block(width),
            row_block(width),
        ],
        out_specs=[row_block(columns // 2), row_block(columns // 2)],
        out_shape=[jax.ShapeDtypeStruct((total, columns // 2), LOW)] * 2,
        compiler_params=pltpu.CompilerParams(vmem_limit_bytes=48 << 20),
        name="heads",
    )(packed, gains, cosine, sine)


def split_heads_back(packed, gains, cosine, sine, queries_grad, pairs_grad, rows):
    total, columns = packed.shape
    width = cosine.shape[1]
    row_block = lambda size: pl.BlockSpec((rows, size), lambda i: (i, 0))
    return pl.pallas_call(
        heads_back_kernel,
        grid=(total // rows,),
        in_specs=[
            row_block(columns),
            pl.BlockSpec((2, width), lambda i: (0, 0)),
            row_block(width),
            row_block(width),
            row_block(columns // 2),
            row_block(columns // 2),
        ],
        out_specs=[row_block(columns), pl.BlockSpec((2, width), lambda i: (0, 0))],
        out_shape=[
            jax.ShapeDtypeStruct((total, columns), LOW),
            jax.ShapeDtypeStruct((2, width), WIDE),
        ],
        compiler_params=pltpu.CompilerParams(vmem_limit_bytes=48 << 20),
        name="heads_back",
    )(packed, gains, cosine, sine, queries_grad, pairs_grad)


def block_weights(offsets, queries, keys, scale):
    scores = (
        lax.dot_general(queries, keys, (((1,), (1,)), ((), ())), preferred_element_type=WIDE)
        * scale
    )
    rows, window = offsets.shape[0], keys.shape[0]
    shape = (rows, window)
    back = (
        lax.broadcasted_iota(jnp.int32, shape, 0)
        + LONGEST
        - lax.broadcasted_iota(jnp.int32, shape, 1)
    )
    allowed = (back >= 0) & (back <= offsets)
    allowed = jnp.concatenate([allowed.astype(WIDE)] * (queries.shape[0] // rows), axis=0) > 0.5
    scores = jnp.where(allowed, scores, NEGATIVE)
    weights = jnp.exp(scores - jnp.max(scores, axis=-1, keepdims=True))
    return weights * (1 / jnp.sum(weights, axis=-1, keepdims=True))


def over(values):
    width = values.shape[1] // 2
    return jnp.concatenate([values[:, :width], values[:, width:]], axis=0)


def beside(values):
    rows = values.shape[0] // 2
    return jnp.concatenate([values[:rows], values[rows:]], axis=1)


def attend_kernel(scale, offsets_ref, queries_ref, pairs_ref, out_ref):
    rows, width = queries_ref.shape[0], queries_ref.shape[1] // 2
    low = pl.multiple_of(pl.program_id(1) * rows, rows)
    pairs = pairs_ref[pl.ds(low, LONGEST + rows), :]
    keys, values = pairs[:, :width], pairs[:, width:]
    shape = (rows, pairs.shape[0])
    back = (
        lax.broadcasted_iota(jnp.int32, shape, 0)
        + LONGEST
        - lax.broadcasted_iota(jnp.int32, shape, 1)
    )
    allowed = (back >= 0) & (back <= offsets_ref[...])
    results = []
    for head in range(2):
        queries = queries_ref[:, head * width : (head + 1) * width]
        scores = lax.dot_general(
            queries, keys, (((1,), (1,)), ((), ())), preferred_element_type=WIDE
        )
        scores = jnp.where(allowed, scores, NEGATIVE)
        weights = jnp.exp((scores - jnp.max(scores, axis=-1, keepdims=True)) * scale)
        weights = weights * (1 / jnp.sum(weights, axis=-1, keepdims=True))
        result = jnp.dot(weights.astype(LOW), values, preferred_element_type=WIDE)
        results.append(result.astype(LOW))
    out_ref[...] = jnp.concatenate(results, axis=1)


def attend_back_kernel(
    scale, offsets_ref, queries_ref, pairs_ref, grad_ref, queries_grad_ref, pairs_grad_ref
):
    rows, width = queries_ref.shape[0], queries_ref.shape[1] // 2

    @pl.when(pl.program_id(1) == 0)
    def _():
        pairs_grad_ref[...] = jnp.zeros_like(pairs_grad_ref)

    low = pl.multiple_of(pl.program_id(1) * rows, rows)
    window = pl.ds(low, LONGEST + rows)
    queries, grad = over(queries_ref[...]), over(grad_ref[...])
    pairs = pairs_ref[window, :]
    keys, values = pairs[:, :width], pairs[:, width:]
    weights = block_weights(offsets_ref[...], queries, keys, scale)
    flow = lax.dot_general(grad, values, (((1,), (1,)), ((), ())), preferred_element_type=WIDE)
    inner = jnp.sum(weights * flow, axis=-1, keepdims=True)
    score_grad = (weights * (flow - inner)).astype(LOW)
    values_grad = lax.dot_general(
        weights.astype(LOW), grad, (((0,), (0,)), ((), ())), preferred_element_type=WIDE
    )
    keys_grad = lax.dot_general(
        score_grad, queries, (((0,), (0,)), ((), ())), preferred_element_type=WIDE
    )
    pairs_grad_ref[window, :] += jnp.concatenate([keys_grad * scale, values_grad], axis=1)
    queries_grad = jnp.dot(score_grad, keys, preferred_element_type=WIDE) * scale
    queries_grad_ref[...] = beside(queries_grad.astype(LOW))


def attention_specs(queries, pairs, rows, head_width):
    width = 2 * head_width
    grid = (queries.shape[1] // width, queries.shape[0] // rows)
    offsets_spec = pl.BlockSpec((rows, 1), lambda g, i: (i, 0))
    rows_spec = pl.BlockSpec((rows, width), lambda g, i: (i, g))
    pairs_spec = pl.BlockSpec((pairs.shape[0], width), lambda g, i: (0, g))
    return (grid, offsets_spec, rows_spec, pairs_spec)


def attend(offsets, queries, pairs, rows, head_width):
    grid, offsets_spec, rows_spec, pairs_spec = attention_specs(queries, pairs, rows, head_width)
    return pl.pallas_call(
        functools.partial(attend_kernel, head_width ** (-0.5)),
        grid=grid,
        in_specs=[offsets_spec, rows_spec, pairs_spec],
        out_specs=rows_spec,
        out_shape=jax.ShapeDtypeStruct(queries.shape, LOW),
        compiler_params=pltpu.CompilerParams(vmem_limit_bytes=48 << 20),
        name="attend",
    )(offsets[:, None], queries, pairs)


def attend_back(offsets, queries, pairs, grad, rows, head_width):
    grid, offsets_spec, rows_spec, pairs_spec = attention_specs(queries, pairs, rows, head_width)
    return pl.pallas_call(
        functools.partial(attend_back_kernel, head_width ** (-0.5)),
        grid=grid,
        in_specs=[offsets_spec, rows_spec, pairs_spec, rows_spec],
        out_specs=[rows_spec, pairs_spec],
        out_shape=[
            jax.ShapeDtypeStruct(queries.shape, LOW),
            jax.ShapeDtypeStruct(pairs.shape, WIDE),
        ],
        compiler_params=pltpu.CompilerParams(vmem_limit_bytes=48 << 20),
        name="attend_back",
    )(offsets[:, None], queries, pairs, grad)


def whole_rows_of(ref):
    teams, rows, columns = ref.shape
    return ref[...].reshape(teams * rows, columns)


def dot_nt(a, b):
    return lax.dot_general(a, b, (((1,), (1,)), ((), ())), preferred_element_type=WIDE)


def feed_kernel(
    normed_ref, gate_ref, up_ref, outward_ref, gated_ref, raised_ref, hidden_ref, update_ref
):
    normed = normed_ref[...]
    gate = dot_nt(normed, whole_rows_of(gate_ref))
    up = dot_nt(normed, whole_rows_of(up_ref))
    gated_ref[...] = gate.astype(LOW)
    raised_ref[...] = up.astype(LOW)
    hidden = (gate / (1 + jnp.exp(-gate)) * up).astype(LOW)
    hidden_ref[...] = hidden
    update_ref[...] = jnp.dot(
        hidden, whole_rows_of(outward_ref), preferred_element_type=WIDE
    ).astype(LOW)


def feed_back_kernel(
    full_ref,
    gated_ref,
    raised_ref,
    gate_ref,
    up_ref,
    outward_ref,
    gate_grad_ref,
    up_grad_ref,
    update_ref,
    *turned_ref,
):
    if turned_ref:

        @pl.when(pl.program_id(0) == 0)
        def _():
            turned_ref[0][...] = whole_rows_of(outward_ref).T

        hidden_grad = jnp.dot(
            full_ref[...], turned_ref[0][...], preferred_element_type=WIDE
        )
    else:
        hidden_grad = dot_nt(full_ref[...], whole_rows_of(outward_ref))
    gate = gated_ref[...].astype(WIDE)
    up = raised_ref[...].astype(WIDE)
    sigmoid = 1 / (1 + jnp.exp(-gate))
    through = hidden_grad * sigmoid
    gate_grad = (through * up * (1 + gate * (1 - sigmoid))).astype(LOW)
    up_grad = (through * gate).astype(LOW)
    gate_grad_ref[...] = gate_grad
    up_grad_ref[...] = up_grad
    update = jnp.dot(gate_grad, whole_rows_of(gate_ref), preferred_element_type=WIDE)
    update += jnp.dot(up_grad, whole_rows_of(up_ref), preferred_element_type=WIDE)
    update_ref[...] = update.astype(LOW)


def feed_grads_kernel(
    gate_grad_ref, up_grad_ref, hidden_ref, normed_ref, full_ref, out_ref, total_ref
):
    teams, rows, columns = out_ref.shape
    width, step = teams * rows, 128

    def fill(left_ref, right_ref):
        for low in range(0, width, step):
            own = slice(low, min(low + step, width))
            total_ref[own] = lax.dot_general(
                left_ref[:, own],
                right_ref[...],
                (((0,), (0,)), ((), ())),
                preferred_element_type=WIDE,
            )
        out_ref[...] = total_ref[...].astype(LOW).reshape(teams, rows, columns)

    pl.when(pl.program_id(0) == 0)(lambda: fill(gate_grad_ref, normed_ref))
    pl.when(pl.program_id(0) == 1)(lambda: fill(up_grad_ref, normed_ref))
    pl.when(pl.program_id(0) == 2)(lambda: fill(hidden_ref, full_ref))


def kind_spec(pack, k):
    teams, _, rows, columns = pack.shape
    return pl.BlockSpec((teams, None, rows, columns), lambda i: (0, k, 0, 0))


def row_spec(rows, columns):
    return pl.BlockSpec((rows, columns), lambda i: (i, 0))


def feed_call(normed, pack, rows):
    total, columns = normed.shape
    width = pack.shape[0] * pack.shape[2]
    wide = jax.ShapeDtypeStruct((total, width), LOW)
    return pl.pallas_call(
        feed_kernel,
        grid=(total // rows,),
        in_specs=[row_spec(rows, columns)] + [kind_spec(pack, k) for k in range(3)],
        out_specs=[row_spec(rows, width)] * 3 + [row_spec(rows, columns)],
        out_shape=[wide] * 3 + [jax.ShapeDtypeStruct((total, columns), LOW)],
        compiler_params=pltpu.CompilerParams(vmem_limit_bytes=48 << 20),
        name="feed",
    )(normed, pack, pack, pack)


def feed_back_call(full, gated, raised, pack, rows, turned):
    total, columns = full.shape
    width = gated.shape[1]
    wide = jax.ShapeDtypeStruct((total, width), LOW)
    return pl.pallas_call(
        feed_back_kernel,
        grid=(total // rows,),
        in_specs=[row_spec(rows, columns)]
        + [row_spec(rows, width)] * 2
        + [kind_spec(pack, k) for k in range(3)],
        out_specs=[row_spec(rows, width)] * 2 + [row_spec(rows, columns)],
        out_shape=[wide] * 2 + [jax.ShapeDtypeStruct((total, columns), LOW)],
        scratch_shapes=[pltpu.VMEM((columns, width), LOW)] if turned else [],
        compiler_params=pltpu.CompilerParams(vmem_limit_bytes=48 << 20),
        name="feed_back",
    )(full, gated, raised, pack, pack, pack)


def feed_grads_call(gate_grad, up_grad, hidden, normed, full, teams):
    total, columns = normed.shape
    width = hidden.shape[1]
    wide_spec = pl.BlockSpec((total, width), lambda k: (0, 0))
    rows_spec = pl.BlockSpec((total, columns), lambda k: (0, 0))
    return pl.pallas_call(
        feed_grads_kernel,
        grid=(3,),
        in_specs=[wide_spec] * 3 + [rows_spec] * 2,
        out_specs=pl.BlockSpec((teams, None, width // teams, columns), lambda k: (0, k, 0, 0)),
        out_shape=jax.ShapeDtypeStruct((teams, 3, width // teams, columns), LOW),
        scratch_shapes=[pltpu.VMEM((width, columns), WIDE)],
        compiler_params=pltpu.CompilerParams(vmem_limit_bytes=58 << 20),
        name="feed_grads",
    )(gate_grad, up_grad, hidden, normed, full)


def local(
    tokens,
    lengths,
    gains,
    qk_gains,
    conv_kernel,
    conv_in,
    conv_out,
    ffn1_in,
    ffn1_out,
    attn_qkv,
    attn_out,
    ffn2_in,
    ffn2_out,
    cotangent,
):
    here = Place()
    depth = here.depth
    stretch = tokens.shape[1]
    slice_width = tokens.shape[2]
    model_width = slice_width * depth
    sections = 2 * here.halves
    stream_rows = sections * stretch
    team_rows = stream_rows // depth
    own_rows = team_rows // RANKS
    head_width = attn_qkv.shape[2] // 4
    groups_here = attn_qkv.shape[1]
    groups = groups_here * depth // RANKS
    block_width = conv_in.shape[0]
    query_rows = min(256, team_rows)
    feed_block = min(512, team_rows)
    spare = depth // RANKS

    def row_goal(k):
        def goal(half, side, z, ring, core):
            part = (z + k) % depth
            rank = part % RANKS
            batch = half * 2 + side
            return (core, rank // 2, batch * spare + part // RANKS, ring, rank % 2)

        return goal

    own_part = (here.z % spare) * RANKS + here.rank

    def row_pieces(values):
        grid = values.reshape(depth, own_rows, slice_width)
        return [
            here.move(
                lax.dynamic_index_in_dim(grid, (here.z + k) % depth, 0, keepdims=False),
                row_goal(k),
            )
            for k in range(depth)
        ]

    def rows_in(pieces):
        columns = here.mirrored(jnp.stack(lax.optimization_barrier(tuple(pieces))), own_part)
        return columns.transpose(1, 0, 2).reshape(own_rows, model_width)

    def rows_out(*arrays):
        count = len(arrays)
        grid = jnp.concatenate(arrays, axis=0).reshape(count * own_rows, depth, slice_width)
        grid = grid.transpose(1, 0, 2)
        pieces = []
        for k in range(depth):
            piece = lax.dynamic_index_in_dim(grid, (own_part - k) % depth, 0, keepdims=False)
            route = [(goal, source) for source, goal in here.route(row_goal(k))]
            pieces.append(lax.ppermute(piece, AXES, route))
        rows = here.rolled(jnp.stack(pieces), here.z)
        rows = rows.reshape(depth, count, own_rows, slice_width).transpose(1, 0, 2, 3)
        return list(rows.reshape(count, 1, stretch, slice_width))

    def inward(values):
        return values.transpose(1, 2, 0)

    def by_square(values):
        kinds, rows, columns = values.shape
        blocks = lax.axis_size(SQUARE)
        parts = values.reshape(kinds, blocks, rows // blocks, columns).transpose(1, 0, 2, 3)
        return parts.reshape(blocks, kinds * (rows // blocks), columns)

    rest = here.rings * depth
    teams = here.halves * rest

    def split_kinds(values, kinds):
        grid = values.reshape(here.halves, rest, kinds, -1, model_width)
        return [grid[:, :, k].reshape(-1, model_width) for k in range(kinds)]

    def halves_sum(grads, *due):
        grids = [grad.astype(LOW).reshape(here.halves, rest, -1, model_width) for grad in grads]
        return here.scatter_half(
            jnp.concatenate(grids, axis=2).reshape(here.halves, -1, model_width), *due
        )

    taps = conv_kernel.shape[0]
    square = lax.axis_index(SQUARE)
    share = slice_width // lax.axis_size(SQUARE)
    channels = teams * share

    heads_rows = attn_out.shape[0] // groups_here
    heads_size = attn_qkv.shape[2] + heads_rows

    def heads_goal(half, side, z, ring, core):
        rank = z // spare
        return (half, rank // 2, (2 * side + core) * spare + z % spare, ring, rank % 2)

    heads_part = jnp.concatenate(
        [inward(attn_qkv), attn_out.reshape(groups_here, heads_rows, -1)], axis=1
    )
    heads_flat = heads_part.shape[0] * heads_part.shape[1]
    heads_moved = here.move(heads_part.reshape(heads_flat, block_width), heads_goal)

    def heads_unpack(gathered):
        blocks = gathered.reshape(
            here.halves, here.rings, 2, 2, spare, groups_here * heads_size, block_width
        )
        ordered = [
            blocks[half, ring, side, core].reshape(groups * heads_size, block_width)
            for half in range(here.halves)
            for side in range(2)
            for ring in range(here.rings)
            for core in range(2)
        ]
        weights = jnp.concatenate(ordered, axis=1).reshape(groups, heads_size, model_width)
        return (
            weights[:, : heads_size - heads_rows].reshape(-1, model_width),
            weights[:, heads_size - heads_rows :].reshape(-1, model_width),
        )

    def heads_rows_of(inward_grad, outward_grad):
        grad = jnp.concatenate(
            [
                inward_grad.astype(LOW).reshape(groups, -1, model_width),
                outward_grad.astype(LOW).reshape(groups, -1, model_width),
            ],
            axis=1,
        ).reshape(groups * heads_size, model_width)
        blocks = [
            grad[:, block_width * k : block_width * (k + 1)]
            for k in range(model_width // block_width)
        ]
        ordered = [
            blocks[((half * 2 + side) * here.rings + ring) * 2 + core]
            for half in range(here.halves)
            for ring in range(here.rings)
            for side in range(2)
            for core in range(2)
        ]
        return jnp.concatenate(ordered, axis=0)

    mixer_flat = 4 * share
    feed_rows = 3 * ffn1_out.shape[0] // lax.axis_size(SQUARE)
    mixer_whole = here.whole_columns(
        by_square(jnp.concatenate([inward(conv_in), conv_out[None]], axis=0))
    )
    residual = rows_in(row_pieces(after(tokens, mixer_whole)))
    own_taps = lax.dynamic_slice_in_dim(conv_kernel, square * share, share, 1)
    own_taps = jnp.pad(own_taps, ((0, 16 - taps), (0, model_width - share)))
    mixer_teams = here.gather_teams(jnp.concatenate([mixer_whole, own_taps], axis=0))
    feed_packs = [
        by_square(jnp.concatenate([inward(inner), outer[None]], axis=0))
        for inner, outer in ((ffn1_in, ffn1_out), (ffn2_in, ffn2_out))
    ]
    feed_parts = here.whole_columns(after(jnp.concatenate(feed_packs, axis=1), mixer_whole))
    mixer_part = mixer_teams.reshape(here.halves, rest, -1, model_width)
    mixer_weights = jnp.concatenate(
        split_kinds(mixer_part[:, :, :mixer_flat].reshape(-1, model_width), 4), axis=0
    )
    mixer_inward, mixer_outward = mixer_weights[: 3 * channels], mixer_weights[3 * channels :]
    kernel = (
        mixer_part[:, :, mixer_flat : mixer_flat + taps, :share]
        .transpose(2, 0, 1, 3)
        .reshape(taps, channels)
        .astype(WIDE)
    )

    aligned = feed_rows % 48 == 0
    out_rows = feed_rows // 3

    def feed_pack(gathered):
        pack = gathered.reshape(-1, 3, out_rows, model_width)
        if aligned:
            return pack
        return pack.transpose(1, 0, 2, 3).reshape(1, 3, -1, model_width)

    def feed_teams_of(grad):
        if not aligned:
            grad = grad.reshape(3, -1, out_rows, model_width).transpose(1, 0, 2, 3)
        return grad.reshape(-1, model_width)

    first_rest = here.gather_rest(after(feed_parts[:feed_rows], mixer_teams, residual))
    first_pack = feed_pack(first_rest)

    own_lengths = jnp.where(here.half == here.core, lengths[0], here.to_rank(lengths[0], 1))
    places = here.z * team_rows + jnp.arange(team_rows + 2, dtype=jnp.int32)
    passed = (places[:, None] >= jnp.cumsum(own_lengths)[None, :]).astype(jnp.int32)
    offsets = places - jnp.sum(passed * own_lengths[None, :], axis=1)
    first_mask = (offsets >= 1).astype(WIDE)[:, None]
    second_mask = (offsets >= 2).astype(WIDE)[:, None]
    offsets = offsets[:team_rows]
    cosine_rows, sine_rows = angles(offsets, head_width)
    beside_gains = here.to_rank(gains, 2)
    half_gains = jnp.where(
        here.side == 0,
        jnp.concatenate([gains, beside_gains]),
        jnp.concatenate([beside_gains, gains]),
    )
    all_gains = half_gains
    if here.halves > 1:
        other_gains = here.to_half(half_gains)
        all_gains = jnp.where(
            here.half == 0,
            jnp.concatenate([half_gains, other_gains]),
            jnp.concatenate([other_gains, half_gains]),
        )
    pair_gains = jnp.tile(qk_gains, (1, 2))

    def gather_ordered(values, *due):
        return jnp.concatenate(here.by_rank(here.gather_rows(values, *due)), axis=0)

    def gather_any(values, *due):
        return jnp.concatenate(here.gather_rows(values, *due), axis=0)

    def scatter_ordered(values, waiting=(), due=()):
        grid = values.astype(LOW).reshape(RANKS, own_rows, model_width)
        blocks = [
            lax.dynamic_index_in_dim(grid, jnp.bitwise_xor(here.rank, k), 0, keepdims=False)
            for k in range(RANKS)
        ]
        return here.scatter_rows(blocks, waiting, due)

    def scatter_any(values, waiting=(), due=()):
        grid = values.astype(LOW).reshape(RANKS, own_rows, model_width)
        return here.scatter_rows([grid[k] for k in range(RANKS)], waiting, due)

    def joined(residual, update):
        return (residual.astype(WIDE) + update).astype(LOW)

    def mixer_forward(residual):
        normed = gather_ordered(root_norm(residual.astype(WIDE), all_gains[0]).astype(LOW))
        projected = times_rows(normed, mixer_inward)
        before, gate, behind = (
            projected[:, :channels],
            projected[:, channels : 2 * channels],
            projected[:, 2 * channels :],
        )
        product = before * behind
        tail = here.up(product[-2:], 1)
        extended = jnp.concatenate([tail, product], axis=0)
        once = extended[1:-1] * first_mask[:team_rows]
        twice = extended[:-2] * second_mask[:team_rows]
        mixed = kernel[2] * product + kernel[1] * once + kernel[0] * twice
        gated = (gate * mixed).astype(LOW)
        update, _ = scatter_ordered(times(gated, mixer_outward))
        return joined(residual, update), (
            residual, normed, before, gate, behind, product, once, twice, mixed, gated,
        )

    def mixer_backward(arriving, saved, *due):
        residual, normed, before, gate, behind, product, once, twice, mixed, gated = saved
        full = gather_ordered(arriving, *due)
        gated_grad = times_rows(full, mixer_outward)
        gate_grad = gated_grad * mixed
        mixed_grad = gated_grad * gate
        following = here.up(mixed_grad[:2], -1)
        extended = jnp.concatenate([mixed_grad, following], axis=0)
        product_grad = (
            kernel[2] * mixed_grad
            + kernel[1] * extended[1:-1] * first_mask[1:-1]
            + kernel[0] * extended[2:] * second_mask[2:]
        )
        kernel_grad = jnp.stack(
            [
                jnp.sum(mixed_grad * twice, axis=0),
                jnp.sum(mixed_grad * once, axis=0),
                jnp.sum(mixed_grad * product, axis=0),
            ]
        )
        low = jnp.concatenate(
            [product_grad * behind, gate_grad, product_grad * before], axis=1
        ).astype(LOW)
        update, (low, full) = scatter_ordered(times(low, mixer_inward), (low, full))
        grad = [columns_times(low[:, k * channels : (k + 1) * channels], normed) for k in range(3)]
        grad.append(columns_times(gated, full))
        leaving, gain_grad = root_norm_back(residual, all_gains[0], update, arriving)
        return leaving, gain_grad, kernel_grad, grad, low

    def square_rows(values, *due):
        return jnp.concatenate(here.gather_square(values, *due), axis=0)

    def square_sums(values, waiting=(), due=()):
        return here.scatter_square(values.astype(LOW), waiting, due)

    def feed_forward(residual, gain_row, pack, gather, *due):
        normed = gather(root_norm(residual.astype(WIDE), gain_row).astype(LOW), *due)
        gated, raised, hidden, update = feed_call(normed, pack, feed_block)
        return update, (residual, normed, gated, raised, hidden)

    def feed_joined(residual, update, scatter, due=()):
        return joined(residual, scatter(update, (), due)[0])

    def feed_backward(arriving, saved, gain_row, pack, gather, scatter, *due):
        residual, normed, gated, raised, hidden = saved
        full = gather(arriving, *due)
        square = full.shape[0] > team_rows
        gate_grad, up_grad, update = feed_back_call(
            full, gated, raised, pack, query_rows if square else feed_block, square
        )
        update, (gate_grad, up_grad, full) = scatter(update, (gate_grad, up_grad, full))
        grad = feed_grads_call(gate_grad, up_grad, hidden, normed, full, pack.shape[0])
        update = after(update, grad)
        leaving, gain_grad = root_norm_back(residual, gain_row, update, arriving)
        return leaving, gain_grad, feed_teams_of(grad)

    halo_steps = LONGEST // team_rows

    def heads_forward(residual, due):
        normed = root_norm(residual.astype(WIDE), all_gains[2]).astype(LOW)
        normed = gather_ordered(normed, *due[0])
        packed = times_rows(normed, heads_inward)
        queries, pairs = split_heads(packed, pair_gains, cosine_rows, sine_rows, query_rows)
        window = jnp.concatenate(
            [here.up(pairs, step) for step in range(halo_steps, 0, -1)] + [pairs], axis=0
        )
        window = after(window, *due[1])
        attended = attend(offsets, queries, window, query_rows, head_width)
        update, _ = scatter_ordered(times(attended, heads_outward), (), due[2])
        return joined(residual, update), (residual, normed, packed, queries, window, attended)

    def heads_backward(arriving, saved):
        residual, normed, packed, queries, window, attended = saved
        full = gather_ordered(arriving)
        attended_grad = times_rows(full, heads_outward).astype(LOW)
        queries_grad, pairs_grad = attend_back(
            offsets, queries, window, attended_grad, query_rows, head_width
        )
        own = pairs_grad[LONGEST:]
        for step in range(1, halo_steps + 1):
            low = (halo_steps - step) * team_rows
            moved = here.up(pairs_grad[low : low + team_rows].astype(LOW), -step)
            own = own + moved.astype(WIDE)
        own = own.astype(LOW)
        low, pair_gains_grad = split_heads_back(
            packed, pair_gains, cosine_rows, sine_rows, queries_grad, own, query_rows
        )
        update, (low, full) = scatter_ordered(times(low, heads_inward), (low, full))
        inward_grad = columns_times(low, normed)
        outward_grad = columns_times(attended, full)
        leaving, gain_grad = root_norm_back(residual, all_gains[2], update, arriving)
        width = head_width
        head_gains_grad = jnp.stack(
            [pair_gains_grad[0, :width] + pair_gains_grad[0, width:], pair_gains_grad[1, :width]]
        )
        return leaving, gain_grad, head_gains_grad, inward_grad, outward_grad, own

    residual, mixer_saved = mixer_forward(residual)
    heads_teams = here.gather_teams(after(heads_moved, first_rest, residual))
    heads_inward, heads_outward = heads_unpack(heads_teams)
    update, first_saved = feed_forward(residual, all_gains[1], first_pack, square_rows)
    residual = feed_joined(residual, update, square_sums)
    second_teams = here.gather_teams(after(feed_parts[feed_rows:], heads_teams, update))
    second_pack = feed_pack(second_teams)
    pieces = row_pieces(after(cotangent, residual))
    residual, heads_saved = heads_forward(
        residual, [(heads_inward, heads_outward, *pieces[:1]), pieces[1:2], pieces[2:3]]
    )
    last_update, second_saved = feed_forward(
        residual, all_gains[3], second_pack, gather_any, *pieces[3:]
    )
    flowing = rows_in(pieces)

    flowing, gain3, second_grad = feed_backward(
        flowing, second_saved, all_gains[3], second_pack, gather_any, scatter_any
    )
    flowing, gain2, head_gains_grad, heads_inward_grad, heads_outward_grad, pairs_low = (
        heads_backward(flowing, heads_saved)
    )
    second_sum = here.scatter_teams(after(second_grad, pairs_low))
    output = feed_joined(residual, after(last_update, flowing), scatter_any)
    heads_grad = heads_rows_of(heads_inward_grad, heads_outward_grad)
    heads_half = here.scatter_half(heads_grad.reshape(here.halves, -1, block_width))
    flowing, gain1, first_grad = feed_backward(
        flowing,
        first_saved,
        all_gains[1],
        first_pack,
        square_rows,
        square_sums,
        heads_grad,
    )
    first_sum = here.scatter_rest(after(first_grad, flowing, second_sum))
    flowing, gain0, kernel_grad, mixer_grad, low = mixer_backward(
        flowing, mixer_saved, output
    )
    mixer_half = halves_sum([mixer_grad[k] for k in range(4)])
    output, input_grad = rows_out(output, after(flowing, mixer_half))
    late = [part.reshape(rest, -1, model_width) for part in (heads_half, mixer_half)]
    late_sum = here.scatter_rest(
        after(jnp.concatenate(late, axis=1).reshape(-1, model_width), first_sum)
    )

    heads_route = [(b, a) for a, b in here.route(heads_goal)]
    (second_grad,) = here.whole_rows((after(second_sum, input_grad), 3))
    (first_grad,) = here.whole_rows((after(first_sum, second_grad), 3))
    heads_wide = heads_flat * block_width // model_width
    heads_grad = late_sum[:heads_wide].reshape(heads_flat, block_width)
    heads_grad = lax.ppermute(heads_grad, AXES, heads_route).reshape(heads_part.shape)
    (mixer_grad,) = here.whole_rows((late_sum[heads_wide:], 4))

    def outside(values):
        return values.transpose(2, 0, 1).astype(WIDE)

    kernel_blocks = kernel_grad.reshape(taps, here.halves, 1, here.rings, depth, 1, share)
    sides = (jnp.arange(2) == here.side).astype(WIDE).reshape(2, 1, 1, 1, 1)
    cores = (jnp.arange(2) == here.core).astype(WIDE).reshape(2, 1)
    kernel_whole = (kernel_blocks * sides * cores).transpose(0, 4, 1, 2, 3, 5, 6)
    small = jnp.concatenate(
        [
            jnp.stack([gain0, gain1, gain2, gain3]).reshape(-1),
            kernel_whole.reshape(-1),
            head_gains_grad.reshape(-1),
        ]
    )
    small = here.total(after(small, input_grad))
    gain_size, kernel_size = 4 * model_width, taps * model_width
    return (
        output,
        input_grad,
        small[:gain_size].reshape(4, model_width),
        small[gain_size + kernel_size :].reshape(2, head_width),
        small[gain_size : gain_size + kernel_size].reshape(taps, model_width),
        outside(mixer_grad[:3]),
        mixer_grad[3].astype(WIDE),
        outside(first_grad[:2]),
        first_grad[2].astype(WIDE),
        outside(heads_grad[:, : heads_size - heads_rows]),
        heads_grad[:, heads_size - heads_rows :].reshape(attn_out.shape).astype(WIDE),
        outside(second_grad[:2]),
        second_grad[2].astype(WIDE),
    )


def solution(mesh):
    sections, depth, replicas = mesh.devices.shape
    fine = Mesh(mesh.devices.reshape(sections // 2, 2, depth, replicas // 2, 2), AXES)
    rows = P(SQUARE, None, "depth")
    columns = P("depth", SQUARE)
    heads = P(SQUARE, "depth", None)
    stream = P(("half", "side"), ("ring", "core"), "depth")
    return jax.shard_map(
        local,
        mesh=fine,
        in_specs=(
            stream,
            P(("ring", "core"), None),
            P(("half", "side"), None),
            P(),
            P(None, "depth"),
            rows,
            columns,
            rows,
            columns,
            heads,
            columns,
            rows,
            columns,
            stream,
        ),
        out_specs=(
            stream,
            stream,
            P(),
            P(),
            P(),
            rows,
            columns,
            rows,
            columns,
            heads,
            columns,
            rows,
            columns,
        ),
        check_vma=False,
    )
```
